32 devices in a mesh: dp: 2 (over core), row: 4 (over y, x), col: 4 (over z).
Axes of the slice: x: 2, y: 2, z: 4, core: 2. Of those that a mesh axis runs over, the one named last changes fastest.
Arguments:
- hidden_in: bfloat16 [768, 4, 1024], P('col', 'dp', 'row')
- segments: int32 [4, 1024], P('dp'), may hold values from 0 to 2, as said below
- w_qkv: bfloat16 [3, 12, 49152], P(None, 'row', 'col'), may hold values from -0.21875 to 0.21875
- b_qkv: bfloat16 [3, 768], P(None, 'row'), may hold values from -3 to 3
- w_dense: bfloat16 [12, 49152], P('row', 'col'), may hold values from -2.5 to 2.5
- b_dense: bfloat16 [768], P('col'), may hold values from -2 to 2
- ln1_gain: bfloat16 [768], P('col'), may hold values from 0.25 to 1.75
- ln1_bias: bfloat16 [768], P('col'), may hold values from -2 to 2
- ln2_gain: bfloat16 [768], P('col'), may hold values from 0.25 to 1.75
- ln2_bias: bfloat16 [768], P('col'), may hold values from -2 to 2
- w_in: bfloat16 [768, 3072], P('col', 'row'), may hold values from -0.21875 to 0.21875
- b_in: bfloat16 [3072], P('row'), may hold values from -3 to 3
- w_out: bfloat16 [768, 3072], P('col', 'row'), may hold values from -0.109375 to 0.109375
- b_out: bfloat16 [768], P('col'), may hold values from -2 to 2
- cotangent: bfloat16 [768, 4, 1024], P('col', 'dp', 'row'), may hold values from -6 to 6
Outputs:
- layer_out: bfloat16 [768, 4, 1024], P('col', 'dp', 'row')
- grad_in: float32 [768, 4, 1024], P('col', 'dp', 'row')
- d_w_qkv: float32 [3, 12, 49152], P(None, 'row', 'col')
- d_b_qkv: float32 [3, 768], P(None, 'row')
- d_w_dense: float32 [12, 49152], P('row', 'col')
- d_b_dense: float32 [768], P('col')
- d_ln1_gain: float32 [768], P('col')
- d_ln1_bias: float32 [768], P('col')
- d_ln2_gain: float32 [768], P('col')
- d_ln2_bias: float32 [768], P('col')
- d_w_in: float32 [768, 3072], P('col', 'row')
- d_b_in: float32 [3072], P('row')
- d_w_out: float32 [768, 3072], P('col', 'row')
- d_b_out: float32 [768], P('col')
The draws below stay inside these ranges and needn't reach their ends.
Inputs may be any that keep to these rules, and one draw needn't show every extreme that they name: `segments`: within each sequence of 1024 tokens the segment numbers never fall: 0 on its first 1 to 128 tokens, 2 on its last 1 to 128 tokens, 1 on all between.
All inputs are finite; a program needn't handle non-finite values.
Results may differ from the reference program's by a relative error of at most 0.012.
Values may be sent and summed in bfloat16 or wider, within the bound.
No kernel may reach another device: no remote copies, remote signals or barrier semaphores. Data moves between devices by JAX's collectives and lax.ppermute only.
A program may use at most 128 MiB of HBM per device.

```python
import math
import jax
import jax.numpy as jnp
from jax import lax

D = 768
H = 12
HD = 64
ROT = 16
FF = 3072
SEQ = 1024
SEQUENCES = 4


def draw_hidden_in(key, part):
    key = jax.random.fold_in(key, 11)
    key_rows, key_cols, key_base = jax.random.split(key, 3)
    row_scale = jnp.exp(jax.random.uniform(key_rows, (1, SEQUENCES, SEQ), jnp.float32, -1.15, 1.15))
    ramp = jnp.arange(D, dtype=jnp.float32)[:, None, None] / D - 0.5
    col_scale = jnp.exp(jax.random.uniform(key_cols, (D, 1, 1), jnp.float32, -1.15, 1.15) + math.log(3.0) * ramp)
    base_vals = jax.random.normal(key_base, (D, SEQUENCES, SEQ), jnp.float32)
    return (base_vals * row_scale * col_scale).astype(jnp.bfloat16)


def draw_segments(key, part):
    key = jax.random.fold_in(key, 23)
    key_head, key_tail = jax.random.split(key)
    head_end = 1 + jax.random.randint(key_head, (SEQUENCES, 1), 0, SEQ // 8)
    tail_start = SEQ - 1 - jax.random.randint(key_tail, (SEQUENCES, 1), 0, SEQ // 8)
    places = jnp.arange(SEQ, dtype=jnp.int32)[None, :]
    labels = (places >= head_end).astype(jnp.int32) + (places >= tail_start).astype(jnp.int32)
    return labels


def steps_of(stream_key, dims, shards, low, top_value):
    def one(position, shards_of):
        steps = jax.random.uniform(jax.random.fold_in(jax.random.fold_in(stream_key, 6), position), (shards_of,), jnp.float32, low / len(shards), top_value / len(shards))
        return jnp.repeat(jnp.exp(steps), dims[position] // shards_of).reshape((-1,) + (1,) * (len(dims) - position - 1))

    factor_of = one(*shards[0])
    for cut in shards[1:]:
        factor_of = factor_of * one(*cut)
    return factor_of


def normal_values(stream_key, dims, deviation, limit, pieces=(), held_as=jnp.bfloat16):
    gain = steps_of(stream_key, dims, pieces, -0.22, 0.18) if pieces else 1.0
    result = jax.random.normal(stream_key, dims, jnp.float32) * deviation * gain
    return jnp.minimum(jnp.maximum(result, -limit), limit).astype(held_as)


def setup_inputs(seed: int = 0) -> dict:
    seeds = jax.random.split(jax.random.key(seed), 16)
    hidden_in = draw_hidden_in(jax.random.fold_in(seeds[15], 71), 0)
    segments = draw_segments(jax.random.fold_in(seeds[15], 71), 0)
    w_qkv = normal_values(seeds[2], (3, H, D * HD), D ** -0.5, 0.21875, ((1, 4), (2, 4)))
    b_qkv = normal_values(seeds[3], (3, D), 0.5, 3.0, ((1, 4),))
    w_dense = normal_values(seeds[4], (H, D * HD), (max(D // 128, 1)) ** -0.5, 2.5, ((0, 4), (1, 4)))
    b_dense = normal_values(seeds[5], (D,), 0.3, 2.0, ((0, 4),))
    ln1_gain = jnp.clip(1.0 + 0.15 * jax.random.normal(seeds[6], (D,), jnp.float32), 0.25, 1.75).astype(jnp.bfloat16)
    ln1_bias = normal_values(seeds[7], (D,), 0.3, 2.0, ((0, 4),))
    ln2_gain = jnp.clip(1.0 + 0.15 * jax.random.normal(seeds[8], (D,), jnp.float32), 0.25, 1.75).astype(jnp.bfloat16)
    ln2_bias = normal_values(seeds[9], (D,), 0.3, 2.0, ((0, 4),))
    w_in = normal_values(seeds[10], (D, FF), D ** -0.5, 0.21875, ((0, 4), (1, 4)))
    b_in = normal_values(seeds[11], (FF,), 0.5, 3.0, ((0, 4),))
    w_out = normal_values(seeds[12], (D, FF), FF ** -0.5, 0.109375, ((0, 4), (1, 4)))
    b_out = normal_values(seeds[13], (D,), 0.3, 2.0, ((0, 4),))
    cotangent = normal_values(seeds[14], (D, SEQUENCES, SEQ), 1.0, 6.0, ((0, 4), (1, 2), (2, 4)))
    return {"hidden_in": hidden_in, "segments": segments, "w_qkv": w_qkv, "b_qkv": b_qkv, "w_dense": w_dense, "b_dense": b_dense, "ln1_gain": ln1_gain, "ln1_bias": ln1_bias, "ln2_gain": ln2_gain, "ln2_bias": ln2_bias, "w_in": w_in, "b_in": b_in, "w_out": w_out, "b_out": b_out, "cotangent": cotangent}


EPS = 1e-05
HIGH = lax.Precision.HIGHEST

@jax.custom_vjp
def low(v):
    return lax.optimization_barrier(v.astype(jnp.bfloat16)).astype(jnp.float32)

@jax.custom_vjp
def low_back(v):
    return v

def low_keep(v):
    return (low(v), None)

def low_pass(kept, grad):
    return (grad,)

def back_keep(v):
    return (v, None)

def back_low(kept, grad):
    return (low(grad),)
low.defvjp(low_keep, low_pass)
low_back.defvjp(back_keep, back_low)

def rotate(vector, places):
    half_rot = ROT // 2
    frequency = 10000.0 ** (-jnp.arange(half_rot, dtype=jnp.float32) * 2.0 / ROT)
    angles = places.astype(jnp.float32)[..., None] * frequency
    cosine = jnp.cos(angles)[..., None, :]
    sine_part = jnp.sin(angles)[..., None, :]
    first_half = vector[..., :half_rot]
    second = vector[..., half_rot:ROT]
    return jnp.concatenate([first_half * cosine - second * sine_part, second * cosine + first_half * sine_part, vector[..., ROT:]], axis=-1)

def doc_places(seg_ids):
    positions = jnp.arange(seg_ids.shape[0], dtype=jnp.int32)
    previous = jnp.concatenate([seg_ids[:1], seg_ids[:-1]])
    starts = jnp.where(seg_ids != previous, positions, jnp.zeros_like(positions))
    return positions - lax.cummax(starts, axis=0)

def layer(params, seq_in, seg_ids):
    w_qkv, b_qkv, w_dense, b_dense, gain_one, shift_one, gain_two, shift_two, w_in, b_in, w_out, b_out = params
    centre = seq_in - lax.optimization_barrier(jnp.mean(seq_in, axis=-1, keepdims=True))
    normed = centre * lax.rsqrt(lax.optimization_barrier(jnp.mean(centre * centre, axis=-1, keepdims=True)) + EPS)
    act_one = low(normed * gain_one + shift_one)
    act_two = low(normed * gain_two + shift_two)
    wq_blocks = w_qkv.reshape(3, H, D, HD)
    qkv = low_back(jnp.einsum('td,shdk->tshk', act_one, wq_blocks, precision=HIGH) + b_qkv.reshape(3, H, HD)[None])
    places = doc_places(seg_ids)
    queries = low(rotate(qkv[:, 0], places))
    key_rows = low(rotate(qkv[:, 1], places))
    values = low(qkv[:, 2])
    scores = low_back(jnp.einsum('qhd,khd->hqk', queries, key_rows, precision=HIGH) * HD ** (-0.5))
    positions = jnp.arange(SEQ, dtype=jnp.int32)
    allowed = (positions[None, :] <= positions[:, None]) & (seg_ids[None, :] == seg_ids[:, None])
    scores = jnp.where(allowed[None], scores, -1000000000.0)
    row_max = lax.optimization_barrier(jnp.max(scores, axis=-1, keepdims=True))
    exponent = jnp.exp(scores - row_max)
    attn_probs = low(exponent / lax.optimization_barrier(jnp.sum(exponent, axis=-1, keepdims=True)))
    attended = low_back(low(jnp.einsum('hqk,khd->qhd', attn_probs, values, precision=HIGH)))
    dense_blocks = w_dense.reshape(H, D, HD)
    hidden_pre = low_back(jnp.dot(act_two, w_in, precision=HIGH) + b_in)
    up_act = low(jax.nn.gelu(hidden_pre, approximate=False))
    attn_out = jnp.einsum('thd,hod->to', attended, dense_blocks, precision=HIGH)
    mlp_out = jnp.einsum('tf,of->to', up_act, w_out, precision=HIGH)
    return seq_in + attn_out + b_dense + mlp_out + b_out

def reference(hidden_in, segments, w_qkv, b_qkv, w_dense, b_dense, ln1_gain, ln1_bias, ln2_gain, ln2_bias, w_in, b_in, w_out, b_out, cotangent):
    params = tuple((param.astype(jnp.float32) for param in (w_qkv, b_qkv, w_dense, b_dense, ln1_gain, ln1_bias, ln2_gain, ln2_bias, w_in, b_in, w_out, b_out)))
    seq_inputs = hidden_in.astype(jnp.float32).transpose(1, 2, 0)
    seg_rows = segments.astype(jnp.int32)

    def forward(weights, inputs):
        seq_step = jax.checkpoint(lambda seq_pair: layer(weights, seq_pair[0], seq_pair[1]))
        return lax.map(seq_step, (inputs, seg_rows))
    layer_out, pullback = jax.vjp(forward, params, seq_inputs)
    grads, grad_in = pullback(cotangent.astype(jnp.float32).transpose(1, 2, 0))
    d_w_qkv, d_b_qkv, d_w_dense, d_b_dense, d_ln1_gain, d_ln1_bias, d_ln2_gain, d_ln2_bias, d_w_in, d_b_in, d_w_out, d_b_out = grads
    return (layer_out.transpose(2, 0, 1).astype(jnp.bfloat16), grad_in.transpose(2, 0, 1), d_w_qkv, d_b_qkv, d_w_dense, d_b_dense, d_ln1_gain, d_ln1_bias, d_ln2_gain, d_ln2_bias, d_w_in, d_b_in, d_w_out, d_b_out)
```

```python
from functools import partial

import jax
import jax.numpy as jnp
from jax import lax
from jax.sharding import PartitionSpec as P

D = 768
HD = 64
ROT = 16
EPS = 1e-05
PAD = 16

f32 = jnp.float32
bf16 = jnp.bfloat16


def xor_peers(axis, shift):
    return [(i, i ^ shift) for i in range(lax.axis_size(axis))]


def turn_peers(shift):
    count = lax.axis_size("dp")
    return [(i, (i + shift) % count) for i in range(count)]


def send(x, axis, shift):
    return lax.ppermute(x, axis, xor_peers(axis, shift))


def gather_xor(x, axis):
    return [x] + [send(x, axis, k) for k in range(1, lax.axis_size(axis))]


def spread_peers(round_of, back=False):
    pairs = []
    cols = lax.axis_size("col")
    for dp in range(lax.axis_size("dp")):
        for col in range(cols):
            half, seq = divmod(col ^ round_of, 2)
            target = (dp // 2 * 2 + half) * cols + 2 * (dp % 2) + seq
            pairs.append((dp * cols + col, target))
    return [(b, a) for a, b in pairs] if back else pairs


def pick(flag, first, second):
    return jnp.where(flag, first, second)


def swap_by(code, parts):
    parts = [pick((code & 1) == 1, parts[j ^ 1], parts[j]) for j in range(4)]
    return [pick((code & 2) == 2, parts[j ^ 2], parts[j]) for j in range(4)]


def sum_parts(parts):
    total = parts[0].astype(f32)
    for part in parts[1:]:
        total = total + part.astype(f32)
    return total


def dot(a, b, contract):
    return lax.dot_general(a, b, (contract, ((), ())), preferred_element_type=f32)


def rotate(vector, cosine, sine):
    a, b = vector[..., : ROT // 2, :], vector[..., ROT // 2 : ROT, :]
    return jnp.concatenate(
        [a * cosine - b * sine, b * cosine + a * sine, vector[..., ROT:, :]], axis=-2
    )


def extend(columns, bias):
    high = lax.reduce_precision(bias, 8, 7)
    rows = jnp.stack([high, bias - high]).astype(bf16)
    rows = jnp.pad(rows, ((0, PAD - 2), (0, 0)))
    return jnp.concatenate([columns.astype(bf16), rows], axis=0)


def body(
    hidden_in,
    segments,
    w_qkv,
    b_qkv,
    w_dense,
    b_dense,
    ln1_gain,
    ln1_bias,
    ln2_gain,
    ln2_bias,
    w_in,
    b_in,
    w_out,
    b_out,
    cotangent,
):
    width, seqs, span = hidden_in.shape
    half_span = span // 2
    cols, rows, dps = lax.axis_size("col"), lax.axis_size("row"), lax.axis_size("dp")
    seq_len = span * rows
    heads = w_qkv.shape[1]
    hw = heads * HD
    ff = w_in.shape[1]
    scale = HD ** (-0.5)
    core = lax.axis_index("dp") % 2
    row = lax.axis_index("row")
    col = lax.axis_index("col")
    first_core = core == 0
    crossed = (core ^ (col >> 1)) == 1
    block = width + PAD

    both = jnp.stack([hidden_in, cotangent])
    pieces = [both[:, :, j % 2, (j // 2) * half_span : (j // 2 + 1) * half_span] for j in range(4)]
    sent = swap_by(col, pieces)
    got = [lax.ppermute(sent[k], ("dp", "col"), spread_peers(k)) for k in range(4)]
    got = [pick(crossed, got[k ^ 2], got[k]) for k in range(4)]
    mine = jnp.concatenate(got, axis=1)
    tokens = jnp.concatenate(gather_xor(mine, "row"), axis=2)

    counts = jnp.stack([jnp.sum(segments < 1, axis=1), jnp.sum(segments < 2, axis=1)], axis=1).astype(f32)
    counts_other = send(counts, "dp", 1)
    counts = pick((col >> 1) == core, counts, counts_other)
    counts = pick((col & 1) == 1, counts[1], counts[0]).astype(jnp.int32)

    gain1, shift1 = ln1_gain.astype(f32), ln1_bias.astype(f32)
    gain2, shift2 = ln2_gain.astype(f32), ln2_bias.astype(f32)
    wq = w_qkv.reshape(3, heads, width, HD).transpose(2, 0, 1, 3).reshape(width, 3 * hw)
    wd = w_dense.reshape(heads, width, HD).transpose(1, 0, 2).reshape(width, hw)
    wq32 = wq.astype(f32)
    bias_q = jnp.sum(wq32 * shift1[:, None], axis=0) + b_qkv.astype(f32).reshape(-1) / cols
    chunk1 = extend(
        jnp.concatenate([wq32 * gain1[:, None], wd.astype(f32)], axis=1),
        jnp.concatenate([bias_q, jnp.zeros((hw,), f32)]),
    )
    part = ff // 2
    own_in = lax.dynamic_slice_in_dim(w_in, core * part, part, 1).astype(f32)
    own_out = lax.dynamic_slice_in_dim(w_out, core * part, part, 1)
    own_b = lax.dynamic_slice_in_dim(b_in, core * part, part, 0).astype(f32)
    bias_f = jnp.sum(own_in * shift2[:, None], axis=0) + own_b / cols
    chunk2 = extend(
        jnp.concatenate([own_in * gain2[:, None], own_out.astype(f32)], axis=1),
        jnp.concatenate([bias_f, jnp.zeros((part,), f32)]),
    )
    own1 = pick(first_core, chunk1[:, : 2 * hw], chunk1[:, 2 * hw :])
    own1 = jnp.concatenate(gather_xor(own1, "col"), axis=0)
    other1 = send(own1, "dp", 1)
    w_qk = pick(first_core, own1, other1)
    w_vd = pick(first_core, other1, own1)
    own2 = jnp.concatenate(gather_xor(chunk2, "col"), axis=0)
    other2 = send(own2, "dp", 1)

    x = tokens[0].astype(f32)
    mean = jnp.mean(x, axis=0, keepdims=True)
    centre = x - mean
    rstd = lax.rsqrt(jnp.mean(centre * centre, axis=0, keepdims=True) + EPS)
    count = x.shape[1]
    normed = (centre * rstd).astype(bf16).reshape(cols, width, count)
    ones = jnp.broadcast_to((jnp.arange(PAD) < 2).astype(bf16)[None, :, None], (cols, PAD, count))
    xn = jnp.concatenate([normed, ones], axis=1).reshape(cols * block, count)
    cot = tokens[1].reshape(cols, width, count)
    cot = jnp.concatenate([cot, jnp.zeros((cols, PAD, count), bf16)], axis=1).reshape(cols * block, count)

    base = jnp.arange(half_span, dtype=jnp.int32)
    def positions(core_of):
        return jnp.concatenate([(row ^ j) * span + core_of * half_span + base for j in range(rows)])
    q_pos = positions(core)
    k_pos = jnp.concatenate([q_pos, positions(1 - core)])
    q_start = jnp.where(q_pos >= counts[1], counts[1], jnp.where(q_pos >= counts[0], counts[0], 0))
    frequency = 10000.0 ** (-jnp.arange(ROT // 2, dtype=f32) * 2.0 / ROT)
    angles = (q_pos - q_start).astype(f32)[None, :] * frequency[:, None]
    cosine, sine = jnp.cos(angles), jnp.sin(angles)

    qk = dot(w_qk, xn, ((0,), (0,))).reshape(2, heads, HD, count)
    qk = rotate(qk, cosine, sine).astype(bf16)
    vals = dot(w_vd[:, :hw], xn, ((0,), (0,))).astype(bf16).reshape(heads, HD, count)
    queries = qk[0]
    kv = jnp.stack([qk[1], vals])
    kv_other = send(kv, "dp", 1)
    keys, values = jnp.concatenate([kv, kv_other], axis=3)
    grad_att = dot(w_vd[:, hw:], cot, ((0,), (0,))).astype(bf16).reshape(heads, HD, count)

    allowed = (k_pos[:, None] <= q_pos[None, :]) & (k_pos[:, None] >= q_start[None, :])
    scores = jnp.einsum("hdk,hdq->hkq", keys, queries, preferred_element_type=f32) * scale
    scores = jnp.where(allowed[None], scores, -1000000000.0)
    top = jnp.max(scores, axis=1, keepdims=True)
    exponent = jnp.exp(scores - top)
    probs = exponent / jnp.sum(exponent, axis=1, keepdims=True)
    probs_low = probs.astype(bf16)
    attended = jnp.einsum("hdk,hkq->hdq", values, probs_low, preferred_element_type=f32).astype(bf16)
    grad_probs = jnp.einsum("hdk,hdq->hkq", values, grad_att, preferred_element_type=f32)
    grad_scores = probs * (grad_probs - jnp.sum(grad_probs * probs, axis=1, keepdims=True))
    scores_low = (grad_scores * scale).astype(bf16)
    grad_q = jnp.einsum("hdk,hkq->hdq", keys, scores_low, preferred_element_type=f32)
    grad_k = jnp.einsum("hdq,hkq->hdk", queries, scores_low, preferred_element_type=f32)
    grad_v = jnp.einsum("hdq,hkq->hdk", grad_att, probs_low, preferred_element_type=f32)
    grad_kv = jnp.stack([grad_k, grad_v])
    grad_kv = grad_kv[..., :count] + send(grad_kv[..., count:].astype(bf16), "dp", 1).astype(f32)
    attended = attended.reshape(hw, count)

    def feed(weights):
        pre = dot(weights[:, :part], xn, ((0,), (0,)))
        up, back = jax.vjp(partial(jax.nn.gelu, approximate=False), pre)
        up = up.astype(bf16)
        grad_up = dot(weights[:, part:], cot, ((0,), (0,)))
        grad_pre = back(grad_up)[0].astype(bf16)
        out = dot(weights[:, part:], up, ((1,), (0,)))
        grad_norm = dot(weights[:, :part], grad_pre, ((1,), (0,)))
        moments = jnp.concatenate(
            [dot(xn, grad_pre, ((1,), (1,))), dot(cot, up, ((1,), (1,)))], axis=1
        ).astype(bf16)
        return out, grad_norm, moments

    out_a, norm_a, mom_a = feed(own2)
    out_b, norm_b, mom_b = feed(other2)

    def scatter_moments(keep, give):
        total = sum_parts([keep, send(give, "dp", 1)]).astype(bf16).reshape(cols, block, -1)
        total = sum_parts([total[0]] + [send(total[k], "col", k) for k in range(1, cols)])
        own = total.astype(bf16)
        for k in range(2, dps, 2):
            total = total + lax.ppermute(own, "dp", turn_peers(k)).astype(f32)
        own = total.astype(bf16)
        other = send(own, "dp", 1)
        return pick(first_core, own, other).astype(f32), pick(first_core, other, own).astype(f32)

    m2_low, m2_high = scatter_moments(mom_a, mom_b)
    m_in = jnp.concatenate([m2_low[:, :part], m2_high[:, :part]], axis=1)
    m_out = jnp.concatenate([m2_low[:, part:], m2_high[:, part:]], axis=1)

    def to_rows(partial_sum):
        low = partial_sum.astype(bf16).reshape(cols, block, count)[:, :width]
        low = [low[..., j * half_span : (j + 1) * half_span] for j in range(rows)]
        return sum_parts([low[0]] + [send(low[j], "row", j) for j in range(1, rows)])

    def to_columns(x):
        x = x.astype(bf16)
        parts = [pick(crossed, x[k ^ 2], x[k]) for k in range(4)]
        parts = [lax.ppermute(parts[k], ("dp", "col"), spread_peers(k, True)) for k in range(4)]
        parts = swap_by(col, parts)
        return jnp.stack(
            [jnp.concatenate([parts[s], parts[2 + s]], axis=1) for s in range(2)], axis=1
        ).astype(f32)

    out_sum = out_a + out_b + dot(w_vd[:, hw:], attended, ((1,), (0,)))
    branch = to_columns(to_rows(out_sum))
    bias_out = b_dense.astype(f32) + b_out.astype(f32)
    layer_out = (hidden_in.astype(f32) + branch + bias_out[:, None, None]).astype(bf16)

    grad_qk = jnp.stack([grad_q, grad_kv[0]])
    grad_qk = rotate(grad_qk, cosine, -sine).astype(bf16).reshape(2 * hw, count)
    grad_val = grad_kv[1].astype(bf16).reshape(hw, count)
    norm_sum = (
        norm_a
        + norm_b
        + dot(w_qk, grad_qk, ((1,), (0,)))
        + dot(w_vd[:, :hw], grad_val, ((1,), (0,)))
    )
    mom_qk = dot(xn, grad_qk, ((1,), (1,))).astype(bf16)
    mom_vd = jnp.concatenate(
        [dot(xn, grad_val, ((1,), (1,))), dot(cot, attended, ((1,), (1,)))], axis=1
    ).astype(bf16)
    m_qk, m_vd = scatter_moments(
        pick(first_core, mom_qk, mom_vd), pick(first_core, mom_vd, mom_qk)
    )
    m_q = jnp.concatenate([m_qk, m_vd[:, :hw]], axis=1)
    m_d = m_vd[:width, hw:]

    grad_normed = to_rows(norm_sum)
    x_row = mine[0].astype(f32).reshape(cols, width, half_span)
    mean_row = jnp.mean(x_row, axis=(0, 1), keepdims=True)
    x_row = x_row - mean_row
    rstd_row = lax.rsqrt(jnp.mean(x_row * x_row, axis=(0, 1), keepdims=True) + EPS)
    n_row = x_row * rstd_row
    grad_x = rstd_row * (
        grad_normed
        - jnp.mean(grad_normed, axis=(0, 1), keepdims=True)
        - n_row * jnp.mean(grad_normed * n_row, axis=(0, 1), keepdims=True)
    )
    grad_in = cotangent.astype(f32) + to_columns(grad_x)

    sum_q, sum_f = m_q[width], m_in[width]
    m_q, m_in, m_out = m_q[:width], m_in[:width], m_out[:width]
    d_wq = m_q * gain1[:, None] + shift1[:, None] * sum_q
    d_w_in = m_in * gain2[:, None] + shift2[:, None] * sum_f
    win32 = w_in.astype(f32)
    small = jnp.stack(
        [
            jnp.sum(wq32 * m_q, axis=1),
            jnp.sum(wq32 * sum_q, axis=1),
            jnp.sum(win32 * m_in, axis=1),
            jnp.sum(win32 * sum_f, axis=1),
            jnp.sum(cotangent.astype(f32), axis=(1, 2)),
        ]
    )
    small = sum_parts(gather_xor(small, "row"))
    d_shared = small[4]
    for k in range(1, dps):
        d_shared = d_shared + lax.ppermute(small[4], "dp", turn_peers(k))
    d_w_qkv = d_wq.reshape(width, 3, heads, HD).transpose(1, 2, 0, 3).reshape(w_qkv.shape)
    d_w_dense = m_d.reshape(width, heads, HD).transpose(1, 0, 2).reshape(w_dense.shape)
    return (
        layer_out,
        grad_in,
        d_w_qkv,
        sum_q.reshape(3, hw),
        d_w_dense,
        d_shared,
        small[0],
        small[1],
        small[2],
        small[3],
        d_w_in,
        sum_f,
        m_out,
        d_shared,
    )


def solution(mesh):
    placed = (
        P("col", "dp", "row"),
        P("dp", None),
        P(None, "row", "col"),
        P(None, "row"),
        P("row", "col"),
        P("col"),
        P("col"),
        P("col"),
        P("col"),
        P("col"),
        P("col", "row"),
        P("row"),
        P("col", "row"),
        P("col"),
        P("col", "dp", "row"),
    )
    return jax.shard_map(
        body,
        mesh=mesh,
        in_specs=placed,
        out_specs=(
            P("col", "dp", "row"),
            P("col", "dp", "row"),
            P(None, "row", "col"),
            P(None, "row"),
            P("row", "col"),
            P("col"),
            P("col"),
            P("col"),
            P("col"),
            P("col"),
            P("col", "row"),
            P("row"),
            P("col", "row"),
            P("col"),
        ),
        check_vma=False,
    )
```

```python
from functools import partial

import jax
import jax.numpy as jnp
from jax import lax
from jax.experimental import pallas as pl
from jax.experimental.pallas import tpu as pltpu
from jax.sharding import PartitionSpec as P

D = 768
HD = 64
ROT = 16
EPS = 1e-05
PAD = 16

f32 = jnp.float32
bf16 = jnp.bfloat16


def xor_peers(axis, shift):
    return [(i, i ^ shift) for i in range(lax.axis_size(axis))]


def turn_peers(shift):
    count = lax.axis_size("dp")
    return [(i, (i + shift) % count) for i in range(count)]


def send(x, axis, shift):
    return lax.ppermute(x, axis, xor_peers(axis, shift))


def send_near(x):
    pairs = []
    cols = lax.axis_size("col")
    for dp in range(lax.axis_size("dp")):
        pairs += [(dp * cols + c, dp * cols + (c ^ (3 - dp % 2))) for c in range(cols)]
    return lax.ppermute(x, ("dp", "col"), pairs)


def gather_xor(x, axis):
    return [x] + [send(x, axis, k) for k in range(1, lax.axis_size(axis))]


def after(x, others):
    return lax.optimization_barrier((x, others))[0]


def spread_peers(round_of, back=False):
    pairs = []
    cols = lax.axis_size("col")
    for dp in range(lax.axis_size("dp")):
        for col in range(cols):
            half, seq = divmod(col ^ round_of, 2)
            target = (dp // 2 * 2 + half) * cols + 2 * (dp % 2) + seq
            pairs.append((dp * cols + col, target))
    return [(b, a) for a, b in pairs] if back else pairs


def pick(flag, first, second):
    return jnp.where(flag, first, second)


def swap_by(code, parts):
    parts = [pick((code & 1) == 1, parts[j ^ 1], parts[j]) for j in range(4)]
    return [pick((code & 2) == 2, parts[j ^ 2], parts[j]) for j in range(4)]


def sum_parts(parts):
    total = parts[0].astype(f32)
    for part in parts[1:]:
        total = total + part.astype(f32)
    return total


def dot(a, b, contract):
    return lax.dot_general(a, b, (contract, ((), ())), preferred_element_type=f32)


def extend(columns, bias):
    high = lax.reduce_precision(bias, 8, 7)
    rows = jnp.stack([high, bias - high]).astype(bf16)
    rows = jnp.pad(rows, ((0, PAD - 2), (0, 0)))
    return jnp.concatenate([columns.astype(bf16), rows], axis=0)


def call(kernel, outs, args, scalars=None):
    specs = [pl.BlockSpec(memory_space=pltpu.VMEM) for _ in args]
    if scalars is not None:
        specs = [pl.BlockSpec(memory_space=pltpu.SMEM)] + specs
        args = [scalars, *args]
    return pl.pallas_call(
        kernel,
        out_shape=outs,
        in_specs=specs,
        out_specs=[pl.BlockSpec(memory_space=pltpu.VMEM) for _ in outs],
        compiler_params=pltpu.CompilerParams(vmem_limit_bytes=48 * 2**20),
        cost_estimate=pl.CostEstimate(flops=0, bytes_accessed=0, transcendentals=0),
    )(*args)


def shaped(shape, dtype):
    return jax.ShapeDtypeStruct(shape, dtype)


def place_kernel(scal, *refs):
    parts, (xn_ref, cot_ref) = refs[:4], refs[4:]
    block = xn_ref.shape[0] // 4
    width, span = parts[0].shape[2:]
    row, crossed = scal[0], scal[2]
    for j in range(4):
        ref = parts[j]
        at = pl.multiple_of((row ^ j) * span, span)
        x = ref[:, 0].astype(f32)
        x = x - jnp.mean(x, axis=(0, 1), keepdims=True)
        x = (x * lax.rsqrt(jnp.mean(x * x, axis=(0, 1), keepdims=True) + EPS)).astype(bf16)
        for k in range(4):
            to = pl.multiple_of((k ^ (2 * crossed)) * block, PAD)
            xn_ref[pl.ds(to, width), pl.ds(at, span)] = x[k]
            cot_ref[pl.ds(to, width), pl.ds(at, span)] = ref[k, 1]
    rest = (lax.broadcasted_iota(jnp.int32, (PAD, xn_ref.shape[1]), 0) < 2).astype(f32).astype(bf16)
    for k in range(4):
        xn_ref[k * block + width : (k + 1) * block, :] = rest
        cot_ref[k * block + width : (k + 1) * block, :] = jnp.zeros_like(rest)


def turn(x, cosine, sine):
    half = ROT // 2
    a, b = x[:half], x[half:ROT]
    return jnp.concatenate([a * cosine - b * sine, b * cosine + a * sine, x[ROT:]], axis=0)


def dot00(a, b):
    return dot(a, b, ((0,), (0,)))


def dot11(a, b):
    return dot(a, b, ((1,), (1,)))


def dot10(a, b):
    return dot(a, b, ((1,), (0,)))


def weight(parts, i, u):
    own, near, near_other, far, far_other = parts
    if i == 3:
        return (far, far_other)[u][...]
    half = far.shape[1]
    side = 1 - u if i == 2 else u
    return (own, near, near_other)[i][:, side * half : (side + 1) * half]


def blocks_of(core, size):
    return [pl.ds(pl.multiple_of(b * size, PAD), size) for b in (0, 3 - core, 2 + core, 1)]


def qkv_kernel(heads, scal, tables, xn, cot, *refs):
    weights, (q_ref, kv_ref, ga_ref) = refs[:5], refs[5:]
    sub = HD // 2
    at_blocks = blocks_of(scal[1], weights[0].shape[0])
    third = heads * sub
    for u in range(2):
        w = [weight(weights, i, u) for i in range(4)]
        pre = sum(dot00(w[i], xn[at_blocks[i], :]) for i in range(4))
        grad = sum(dot00(w[i][:, 2 * 128 :], cot[at_blocks[i], :]) for i in range(4))
        cosine, sine = tables[2 * u], tables[2 * u + 1]
        for h in range(heads):
            dims = slice(u * sub, (u + 1) * sub)
            at = h * sub
            q_ref[h, dims, :] = turn(pre[at : at + sub], cosine, sine).astype(bf16)
            at += third
            kv_ref[0, h, dims, :] = turn(pre[at : at + sub], cosine, sine).astype(bf16)
            at += third
            kv_ref[1, h, dims, :] = pre[at : at + sub].astype(bf16)
            at += third - 2 * 128
            ga_ref[h, dims, :] = grad[at : at + sub].astype(bf16)


def put_sums(keep, give, i, u, value):
    half = value.shape[1]
    if i == 1:
        keep[:, u * half : (u + 1) * half] = value
    elif i == 2:
        give[:, (1 - u) * half : (2 - u) * half] = value
    else:
        at = (2 if i == 3 else 3) * half
        (keep, give)[u][:, at : at + half] = value


def swapped(x):
    sub = HD // 2
    return jnp.concatenate([x[sub:], x[:sub]], axis=0)


def attention_kernel(
    span, scal, start, q_ref, kv_ref, kv_other, ga_ref, att_ref, gq_ref, gkv_ref, gkv_other, kc, vc, gk, gv
):
    count = q_ref.shape[2]
    rows = 2 * count // span
    half = span // 2
    core = scal[1]
    for rr in range(rows):
        mine, lanes = slice(rr * half, (rr + 1) * half), rr * span
        for ref, at in ((kc, 0), (vc, 1)):
            ref[:, lanes : lanes + half] = kv_ref[at, 0, :, mine]
            ref[:, lanes + half : lanes + span] = swapped(kv_other[at, 0, :, mine])
    kt, vt = kc[...].T, vc[...].T
    gk[...] = jnp.zeros_like(gk)
    gv[...] = jnp.zeros_like(gv)
    scale = HD ** (-0.5)
    for a in range(rows):
        size = (a + 1) * span
        mine = slice(a * half, (a + 1) * half)
        q, ga = q_ref[0, :, mine], ga_ref[0, :, mine]
        key = lax.broadcasted_iota(jnp.int32, (size, 1), 0)
        at = key % span
        key = key - at + jnp.where((at >= half) == (core == 0), half, 0) + at % half
        query = lax.broadcasted_iota(jnp.int32, (1, half), 1) + (a * span + core * half)
        first = start[:, mine]
        allowed = (key <= query) & (key >= first)
        scores = jnp.where(allowed, dot10(kt[:size], q) * scale, -1000000000.0)
        top = jnp.max(scores, axis=0, keepdims=True)
        exponent = jnp.exp(scores - top)
        probs = exponent * (1.0 / jnp.sum(exponent, axis=0, keepdims=True))
        low = probs.astype(bf16)
        att_ref[0, :, mine] = dot10(vc[:, :size], low).astype(bf16)
        grad = dot10(vt[:size], ga)
        total = jnp.sum(grad * probs, axis=0, keepdims=True)
        grad = (probs * (grad - total) * scale).astype(bf16)
        gq_ref[0, :, mine] = dot10(kc[:, :size], grad)
        gk[:, :size] += dot11(q, grad)
        gv[:, :size] += dot11(ga, low)
    for rr in range(rows):
        mine, lanes = slice(rr * half, (rr + 1) * half), rr * span
        for ref, at in ((gk, 0), (gv, 1)):
            gkv_ref[at, 0, :, mine] = ref[:, lanes : lanes + half]
            gkv_other[at, 0, :, mine] = ref[:, lanes + half : lanes + span].astype(bf16)


def qkv_grad_kernel(heads, scal, tables, gq_ref, gkv_ref, gk_other, gv_other, att_ref, xn, cot, *outs):
    sub = HD // 2
    third = heads * sub
    keep, give = outs[4:]
    at_blocks = blocks_of(scal[1], keep.shape[0])
    zeros = jnp.zeros((third, xn.shape[1]), bf16)
    for u in range(2):
        grads_ref, att_out = outs[2 * u : 2 * u + 2]
        cosine, sine = tables[2 * u], tables[2 * u + 1]
        dims = slice(u * sub, (u + 1) * sub)
        swap = slice((1 - u) * sub, (2 - u) * sub)
        for h in range(heads):
            at = h * sub
            grads_ref[at : at + sub, :] = turn(gq_ref[h, dims, :], cosine, -sine).astype(bf16)
            g = gkv_ref[0, h, dims, :] + gk_other[0, h, swap, :].astype(f32)
            at += third
            grads_ref[at : at + sub, :] = turn(g, cosine, -sine).astype(bf16)
            g = gkv_ref[1, h, dims, :] + gv_other[0, h, swap, :].astype(f32)
            at += third
            grads_ref[at : at + sub, :] = g.astype(bf16)
            at += third
            att_out[at : at + sub, :] = att_ref[h, dims, :]
        grads_ref[3 * third :, :] = zeros
        for s in range(3):
            att_out[s * third : (s + 1) * third, :] = zeros
        for i in range(4):
            total = dot11(xn[at_blocks[i], :], grads_ref[...]) + dot11(cot[at_blocks[i], :], att_out[...])
            put_sums(keep, give, i, u, total.astype(bf16))


def feed_kernel(scal, xn, cot, *refs):
    weights, acts, (keep, give) = refs[:5], refs[5:9], refs[9:]
    at_blocks = blocks_of(scal[1], weights[0].shape[0])
    part = acts[0].shape[0]
    for u in range(2):
        up_ref, grad_ref = acts[2 * u : 2 * u + 2]
        w = [weight(weights, i, u) for i in range(4)]
        pre = sum(dot00(w[i][:, :part], xn[at_blocks[i], :]) for i in range(4))
        phi = 0.5 * (1.0 + lax.erf(pre * (0.5**0.5)))
        slope = phi + pre * (jnp.exp(-0.5 * pre * pre) * 0.3989422804014327)
        up_ref[...] = (pre * phi).astype(bf16)
        grad = sum(dot00(w[i][:, part:], cot[at_blocks[i], :]) for i in range(4))
        grad_ref[...] = (grad * slope).astype(bf16)
        for i in range(4):
            total = jnp.concatenate(
                [
                    dot11(xn[at_blocks[i], :], grad_ref[...]).astype(bf16),
                    dot11(cot[at_blocks[i], :], up_ref[...]).astype(bf16),
                ],
                axis=1,
            )
            put_sums(keep, give, i, u, total)


def back_kernel(scal, *refs):
    w1, w2, acts, outs = refs[:5], refs[5:10], refs[10:18], refs[18:]
    part = acts[4].shape[0]
    rows, (_, _, width, span) = len(outs), outs[0].shape
    row, core = scal[0], scal[1]
    for i, to in enumerate((0, 3 - core, 2 + core, 1)):
        for way in range(2):
            side = slice((1 - way) * part, (2 - way) * part)
            total = sum(dot10(weight(w1, i, u), acts[2 * way + u][...]) for u in range(2))
            total += sum(dot10(weight(w2, i, u)[:, side], acts[4 + 2 * way + u][...]) for u in range(2))
            total = total[:width].astype(bf16)
            for j, out in enumerate(outs):
                value = total[:, :span]
                for rr in range(1, rows):
                    value = jnp.where((row ^ j) == rr, total[:, rr * span : (rr + 1) * span], value)
                out[to, way] = value


def pair_kernel(*refs):
    near, far, own = refs[4:]
    to = 0
    for keep, got in (refs[:2], refs[2:4]):
        size = keep.shape[1] // 4
        total = keep[...].astype(f32) + got[...].astype(f32)
        near[:, 2 * to : 2 * to + 2 * size] = total[:, : 2 * size].astype(bf16)
        far[:, to : to + size] = total[:, 2 * size : 3 * size].astype(bf16)
        own[:, to : to + size] = total[:, 3 * size :]
        to += size


def total_kernel(near, far, own, out):
    third = far.shape[1] // 3
    for at, size in ((0, third), (third, 2 * third)):
        mine = slice(at, at + size)
        total = near[:, 2 * at : 2 * at + size].astype(f32) + far[:, mine].astype(f32) + own[:, mine]
        out[:, 2 * at : 2 * at + size] = total.astype(bf16)
        out[:, 2 * at + size : 2 * (at + size)] = near[:, 2 * at + size : 2 * (at + size)]


def final_kernel(scal, here, there, scales, wq_ref, win_ref, d_wq, d_wd, d_win, d_wout, d_bq, d_bf, small):
    heads, width, _ = d_wd.shape
    sub = HD // 2
    tail = d_win.shape[1]
    part = tail // 2
    third = heads * sub
    mine_first = scal[1] == 0
    gain1, shift1, gain2, shift2 = (scales[:, i : i + 1] for i in range(4))

    def both(at, size):
        lo, hi = slice(at, at + size), slice(at + size, at + 2 * size)
        mine = here[:, lo].astype(f32) + there[:, hi].astype(f32)
        theirs = here[:, hi].astype(f32) + there[:, lo].astype(f32)
        return jnp.where(mine_first, mine, theirs), jnp.where(mine_first, theirs, mine)

    sums = [jnp.zeros((width, 1), f32) for _ in range(4)]
    for a, m in enumerate(both(0, 4 * third)):
        dims = slice(a * sub, (a + 1) * sub)
        row = m[width : width + 1, : 3 * third]
        w = wq_ref[a].astype(f32)
        sums[0] += jnp.sum(w * m[:width, : 3 * third], axis=1, keepdims=True)
        sums[1] += jnp.sum(w * row, axis=1, keepdims=True)
        d_bq[a : a + 1, :] = row
        grad = m[:width, : 3 * third] * gain1 + shift1 * row
        for s in range(3):
            for h in range(heads):
                at = (s * heads + h) * sub
                d_wq[s, h, :, dims] = grad[:, at : at + sub]
        for h in range(heads):
            at = 3 * third + h * sub
            d_wd[h, :, dims] = m[:width, at : at + sub]
    for a, m in enumerate(both(8 * third, tail)):
        cols = slice(a * part, (a + 1) * part)
        row = m[width : width + 1, :part]
        w = win_ref[:, cols].astype(f32)
        sums[2] += jnp.sum(w * m[:width, :part], axis=1, keepdims=True)
        sums[3] += jnp.sum(w * row, axis=1, keepdims=True)
        d_bf[a : a + 1, :] = row
        d_win[:, cols] = m[:width, :part] * gain2 + shift2 * row
        d_wout[:, cols] = m[:width, part:]
    small[...] = jnp.concatenate(sums, axis=1)


def row_kernel(scal, x_ref, *refs):
    parts, outs = refs[:4], refs[4:]
    crossed = scal[2]
    x = x_ref[:, 0].astype(f32)
    x = x - jnp.mean(x, axis=(0, 1), keepdims=True)
    rstd = lax.rsqrt(jnp.mean(x * x, axis=(0, 1), keepdims=True) + EPS)
    x = x * rstd
    sums = []
    for way in range(2):
        total = sum(p[:, way].astype(f32) for p in parts)
        sums.append([jnp.where(crossed == 1, total[k ^ 2], total[k]) for k in range(4)])
    grad = jnp.stack(sums[1])
    grad = rstd * (
        grad
        - jnp.mean(grad, axis=(0, 1), keepdims=True)
        - x * jnp.mean(grad * x, axis=(0, 1), keepdims=True)
    )
    for k in range(4):
        outs[k][0] = sums[0][k].astype(bf16)
        outs[k][1] = grad[k].astype(bf16)


def body(
    hidden_in,
    segments,
    w_qkv,
    b_qkv,
    w_dense,
    b_dense,
    ln1_gain,
    ln1_bias,
    ln2_gain,
    ln2_bias,
    w_in,
    b_in,
    w_out,
    b_out,
    cotangent,
):
    width, seqs, span = hidden_in.shape
    half_span = span // 2
    cols, rows, dps = lax.axis_size("col"), lax.axis_size("row"), lax.axis_size("dp")
    heads = w_qkv.shape[1]
    hw = heads * HD
    sub = HD // 2
    ff = w_in.shape[1]
    core = lax.axis_index("dp") % 2
    row = lax.axis_index("row")
    col = lax.axis_index("col")
    first_core = core == 0
    crossed = (core ^ (col >> 1)) == 1
    block = width + PAD
    count = rows * half_span

    both = jnp.stack([hidden_in, cotangent])
    pieces = [both[:, :, j % 2, (j // 2) * half_span : (j // 2 + 1) * half_span] for j in range(4)]
    sent = swap_by(col, pieces)
    got = [lax.ppermute(sent[k], ("dp", "col"), spread_peers(k)) for k in range(4)]
    mine = jnp.stack(got)
    tokens = gather_xor(mine, "row")

    counts = jnp.stack([jnp.sum(segments < 1, axis=1), jnp.sum(segments < 2, axis=1)], axis=1).astype(f32)
    counts_other = send(counts, "dp", 1)
    counts = pick((col >> 1) == core, counts, counts_other)
    counts = pick((col & 1) == 1, counts[1], counts[0]).astype(jnp.int32)
    scalars = jnp.stack([row, core, crossed.astype(jnp.int32)])

    gain1, shift1 = ln1_gain.astype(f32), ln1_bias.astype(f32)
    gain2, shift2 = ln2_gain.astype(f32), ln2_bias.astype(f32)

    def in_order(halves):
        low, high = halves
        return jnp.concatenate([pick(first_core, low, high), pick(first_core, high, low)], axis=-1)

    wq = w_qkv.reshape(3, heads, width, 2, sub).transpose(3, 2, 0, 1, 4).reshape(2, width, -1)
    wd = w_dense.reshape(heads, width, 2, sub).transpose(2, 1, 0, 3).reshape(2, width, -1)
    bias_q = b_qkv.reshape(3, heads, 2, sub).transpose(2, 0, 1, 3).reshape(2, -1).astype(f32) / cols
    part = ff // 2
    bias_f = b_in.reshape(2, part).astype(f32) / cols
    halves1, halves2 = [], []
    for u in range(2):
        w = wq[u].astype(f32)
        bias = jnp.sum(w * shift1[:, None], axis=0) + bias_q[u]
        halves1.append(
            extend(
                jnp.concatenate([w * gain1[:, None], wd[u].astype(f32)], axis=1),
                jnp.concatenate([bias, jnp.zeros((heads * sub,), f32)]),
            )
        )
        w = w_in[:, u * part : (u + 1) * part].astype(f32)
        bias = jnp.sum(w * shift2[:, None], axis=0) + bias_f[u]
        halves2.append(
            extend(
                jnp.concatenate([w * gain2[:, None], w_out[:, u * part : (u + 1) * part].astype(f32)], axis=1),
                jnp.concatenate([bias, jnp.zeros((part,), f32)]),
            )
        )

    head, tail = 2 * hw, 2 * part
    own1, own2 = in_order(halves1), in_order(halves2)
    near1 = send_near(after(own1, [sent, counts_other]))
    far = send(jnp.concatenate([own1[:, :head], own2[:, :tail]], axis=1), "col", 1)
    near2 = send_near(after(own2, [near1, far, tokens[1:]]))
    far_other = send(far, "dp", 1)
    w1 = [own1, near1, send(near1, "dp", 1), far[:, :head], far_other[:, :head]]

    base = jnp.arange(half_span, dtype=jnp.int32)
    q_pos = jnp.concatenate([rr * span + core * half_span + base for rr in range(rows)])
    q_start = jnp.where(q_pos >= counts[1], counts[1], jnp.where(q_pos >= counts[0], counts[0], 0))
    frequency = 10000.0 ** (-jnp.arange(ROT // 2, dtype=f32) * 2.0 / ROT)
    angles = (q_pos - q_start).astype(f32)[None, :] * frequency[:, None]
    cosine, sine = jnp.cos(angles), jnp.sin(angles)
    unit, nil = jnp.ones_like(cosine), jnp.zeros_like(sine)
    tables = jnp.stack(
        [
            pick(first_core, cosine, unit),
            pick(first_core, sine, nil),
            pick(first_core, unit, cosine),
            pick(first_core, nil, sine),
        ]
    )

    grid_shape = (cols * block, count)
    xn, cot = call(place_kernel, [shaped(grid_shape, bf16)] * 2, tokens, scalars)
    queries, kv, grad_att = call(
        partial(qkv_kernel, heads),
        [
            shaped((heads, HD, count), bf16),
            shaped((2, heads, HD, count), bf16),
            shaped((heads, HD, count), bf16),
        ],
        [tables, xn, cot, *w1],
        scalars,
    )
    kv_other = send(kv, "dp", 1)

    by_head = pl.BlockSpec((1, HD, count), lambda h: (h, 0, 0))
    by_head2 = pl.BlockSpec((2, 1, HD, count), lambda h: (0, h, 0, 0))
    attended, grad_q, grad_kv, grad_kv_other = pl.pallas_call(
        partial(attention_kernel, span),
        grid=(heads,),
        in_specs=[
            pl.BlockSpec(memory_space=pltpu.SMEM),
            pl.BlockSpec((1, count), lambda h: (0, 0)),
            by_head,
            by_head2,
            by_head2,
            by_head,
        ],
        out_specs=[by_head, by_head, by_head2, by_head2],
        out_shape=[
            shaped((heads, HD, count), bf16),
            shaped((heads, HD, count), f32),
            shaped((2, heads, HD, count), f32),
            shaped((2, heads, HD, count), bf16),
        ],
        scratch_shapes=[
            pltpu.VMEM((HD, 2 * count), bf16),
            pltpu.VMEM((HD, 2 * count), bf16),
            pltpu.VMEM((HD, 2 * count), f32),
            pltpu.VMEM((HD, 2 * count), f32),
        ],
        compiler_params=pltpu.CompilerParams(vmem_limit_bytes=48 * 2**20),
        cost_estimate=pl.CostEstimate(
            flops=0, bytes_accessed=0, transcendentals=0
        ),
    )(scalars, q_start[None, :], queries, kv, kv_other, grad_att)
    grad_kv_got = [send(grad_kv_other[:1], "dp", 1), send(grad_kv_other[1:], "dp", 1)]

    near2 = after(near2, [attended])
    w2 = [own2, near2, send(near2, "dp", 1), far[:, head:], far_other[:, head:]]
    act = shaped((part, count), bf16)
    sums2 = shaped((block, 4 * tail), bf16)
    up_a, hid_a, up_b, hid_b, keep2, give2 = call(
        feed_kernel, [act] * 4 + [sums2] * 2, [xn, cot, *w2], scalars
    )
    got2 = send(give2, "dp", 1)

    half_act = shaped((head, count), bf16)
    sums1 = shaped((block, 4 * head), bf16)
    grads_a, att_a, grads_b, att_b, keep1, give1 = call(
        partial(qkv_grad_kernel, heads),
        [half_act] * 4 + [sums1] * 2,
        [tables, grad_q, grad_kv, *grad_kv_got, after(attended, keep2), xn, cot],
        scalars,
    )
    got1 = send(give1, "dp", 1)
    low_near, low_far, own_sum = call(
        pair_kernel,
        [
            shaped((block, 2 * (head + tail)), bf16),
            shaped((block, head + tail), bf16),
            shaped((block, head + tail), f32),
        ],
        [keep1, got1, keep2, got2],
    )
    sum_near = send_near(low_near)
    sum_far = send(low_far, "col", 1)

    strip = shaped((cols, 2, width, half_span), bf16)
    sums = call(
        back_kernel,
        [strip] * rows,
        [*w1, *w2, *after([att_a, att_b, grads_a, grads_b, up_a, up_b, hid_a, hid_b], [low_near])],
        scalars,
    )
    sums = [sums[0]] + [send(sums[j], "row", j) for j in range(1, rows)]
    piece = shaped((2, width, half_span), bf16)
    back = call(row_kernel, [piece] * cols, [mine, *sums], scalars)
    back = [lax.ppermute(back[k], ("dp", "col"), spread_peers(k, True)) for k in range(4)]
    back = swap_by(col, back)
    branch, grad_x = jnp.stack(
        [jnp.concatenate([back[s], back[2 + s]], axis=2) for s in range(2)], axis=2
    ).astype(f32)
    bias_out = b_dense.astype(f32) + b_out.astype(f32)
    layer_out = (hidden_in.astype(f32) + branch + bias_out[:, None, None]).astype(bf16)
    grad_in = cotangent.astype(f32) + grad_x

    total = call(total_kernel, [shaped((block, 2 * (head + tail)), bf16)], [sum_near, sum_far, own_sum])[0]
    wide = total.astype(f32)
    for k in range(2, dps, 2):
        wide = wide + lax.ppermute(total, "dp", turn_peers(k)).astype(f32)
    total = wide.astype(bf16)
    other = send(total, "dp", 1)

    scales = jnp.stack([gain1, shift1, gain2, shift2], axis=1)
    d_wq, d_wd, d_w_in, d_w_out, d_bq, d_bf, small = call(
        final_kernel,
        [
            shaped((3, heads, width, HD), f32),
            shaped((heads, width, HD), f32),
            shaped((width, ff), f32),
            shaped((width, ff), f32),
            shaped((2, 3 * heads * sub), f32),
            shaped((2, part), f32),
            shaped((width, 4), f32),
        ],
        [total, other, scales, wq, w_in],
        scalars,
    )
    c_sum = jnp.sum(cotangent.astype(f32), axis=(1, 2))
    small = jnp.concatenate([small.T, c_sum[None]])
    small = sum_parts(gather_xor(small, "row"))
    d_shared = small[4]
    for k in range(1, dps):
        d_shared = d_shared + lax.ppermute(small[4], "dp", turn_peers(k))
    return (
        layer_out,
        grad_in,
        d_wq.reshape(w_qkv.shape),
        d_bq.reshape(2, 3, heads, sub).transpose(1, 2, 0, 3).reshape(3, hw),
        d_wd.reshape(w_dense.shape),
        d_shared,
        small[0],
        small[1],
        small[2],
        small[3],
        d_w_in,
        d_bf.reshape(ff),
        d_w_out,
        d_shared,
    )


def solution(mesh):
    placed = (
        P("col", "dp", "row"),
        P("dp", None),
        P(None, "row", "col"),
        P(None, "row"),
        P("row", "col"),
        P("col"),
        P("col"),
        P("col"),
        P("col"),
        P("col"),
        P("col", "row"),
        P("row"),
        P("col", "row"),
        P("col"),
        P("col", "dp", "row"),
    )
    return jax.shard_map(
        body,
        mesh=mesh,
        in_specs=placed,
        out_specs=(
            P("col", "dp", "row"),
            P("col", "dp", "row"),
            P(None, "row", "col"),
            P(None, "row"),
            P("row", "col"),
            P("col"),
            P("col"),
            P("col"),
            P("col"),
            P("col"),
            P("col", "row"),
            P("row"),
            P("col", "row"),
            P("col"),
        ),
        check_vma=False,
    )
```

```python
from functools import partial

import jax
import jax.numpy as jnp
from jax import lax
from jax.experimental import pallas as pl
from jax.experimental.pallas import tpu as pltpu
from jax.sharding import PartitionSpec as P

D = 768
HD = 64
ROT = 16
EPS = 1e-05
PAD = 16

f32 = jnp.float32
bf16 = jnp.bfloat16


def xor_peers(axis, shift):
    return [(i, i ^ shift) for i in range(lax.axis_size(axis))]


def turn_peers(shift):
    count = lax.axis_size("dp")
    return [(i, (i + shift) % count) for i in range(count)]


def send(x, axis, shift):
    return lax.ppermute(x, axis, xor_peers(axis, shift))


def send_near(x):
    pairs = []
    cols = lax.axis_size("col")
    for dp in range(lax.axis_size("dp")):
        pairs += [(dp * cols + c, dp * cols + (c ^ (3 - dp % 2))) for c in range(cols)]
    return lax.ppermute(x, ("dp", "col"), pairs)


def gather_xor(x, axis):
    return [x] + [send(x, axis, k) for k in range(1, lax.axis_size(axis))]


def after(x, others):
    return lax.optimization_barrier((x, others))[0]


def spread_peers(round_of, back=False):
    pairs = []
    cols = lax.axis_size("col")
    for dp in range(lax.axis_size("dp")):
        for col in range(cols):
            half, seq = divmod(col ^ round_of, 2)
            target = (dp // 2 * 2 + half) * cols + 2 * (dp % 2) + seq
            pairs.append((dp * cols + col, target))
    return [(b, a) for a, b in pairs] if back else pairs


def pick(flag, first, second):
    return jnp.where(flag, first, second)


def swap_by(code, parts):
    parts = [pick((code & 1) == 1, parts[j ^ 1], parts[j]) for j in range(4)]
    return [pick((code & 2) == 2, parts[j ^ 2], parts[j]) for j in range(4)]


def sum_parts(parts):
    total = parts[0].astype(f32)
    for part in parts[1:]:
        total = total + part.astype(f32)
    return total


def dot(a, b, contract):
    return lax.dot_general(a, b, (contract, ((), ())), preferred_element_type=f32)


def extend(columns, bias):
    high = lax.reduce_precision(bias, 8, 7)
    rows = jnp.stack([high, bias - high]).astype(bf16)
    rows = jnp.pad(rows, ((0, PAD - 2), (0, 0)))
    return jnp.concatenate([columns.astype(bf16), rows], axis=0)


def call(kernel, outs, args, scalars=None, cost=0):
    specs = [pl.BlockSpec(memory_space=pltpu.VMEM) for _ in args]
    if scalars is not None:
        specs = [pl.BlockSpec(memory_space=pltpu.SMEM)] + specs
        args = [scalars, *args]
    return pl.pallas_call(
        kernel,
        out_shape=outs,
        in_specs=specs,
        out_specs=[pl.BlockSpec(memory_space=pltpu.VMEM) for _ in outs],
        compiler_params=pltpu.CompilerParams(vmem_limit_bytes=48 * 2**20),
        cost_estimate=pl.CostEstimate(flops=cost, bytes_accessed=0, transcendentals=0),
    )(*args)


def shaped(shape, dtype):
    return jax.ShapeDtypeStruct(shape, dtype)


def place_kernel(scal, *refs):
    parts, (xn_ref, cot_ref) = refs[:4], refs[4:]
    block = xn_ref.shape[0] // 4
    width, span = parts[0].shape[2:]
    row, crossed = scal[0], scal[2]
    for j in range(4):
        ref = parts[j]
        at = pl.multiple_of((row ^ j) * span, span)
        x = ref[:, 0].astype(f32)
        x = x - jnp.mean(x, axis=(0, 1), keepdims=True)
        x = (x * lax.rsqrt(jnp.mean(x * x, axis=(0, 1), keepdims=True) + EPS)).astype(bf16)
        for k in range(4):
            to = pl.multiple_of((k ^ (2 * crossed)) * block, PAD)
            xn_ref[pl.ds(to, width), pl.ds(at, span)] = x[k]
            cot_ref[pl.ds(to, width), pl.ds(at, span)] = ref[k, 1]
    rest = (lax.broadcasted_iota(jnp.int32, (PAD, xn_ref.shape[1]), 0) < 2).astype(f32).astype(bf16)
    for k in range(4):
        xn_ref[k * block + width : (k + 1) * block, :] = rest
        cot_ref[k * block + width : (k + 1) * block, :] = jnp.zeros_like(rest)


def turn(x, cosine, sine):
    half = ROT // 2
    a, b = x[:half], x[half:ROT]
    return jnp.concatenate([a * cosine - b * sine, b * cosine + a * sine, x[ROT:]], axis=0)


def dot00(a, b):
    return dot(a, b, ((0,), (0,)))


def dot11(a, b):
    return dot(a, b, ((1,), (1,)))


def dot10(a, b):
    return dot(a, b, ((1,), (0,)))


def weight(parts, i, u):
    half = parts[i].shape[1] // 2
    side = 1 - u if i == 2 else u
    return parts[i][:, side * half : (side + 1) * half]


def blocks_of(core, size):
    return [pl.ds(pl.multiple_of(b * size, PAD), size) for b in (0, 3 - core, 2 + core, 1)]


def qkv_kernel(heads, scal, tables, xn, cot, *refs):
    weights, (q_ref, kv_ref, ga_ref) = refs[:4], refs[4:]
    sub = HD // 2
    at_blocks = blocks_of(scal[1], weights[0].shape[0])
    third = heads * sub
    for u in range(2):
        w = [weight(weights, i, u) for i in range(4)]
        pre = sum(dot00(w[i], xn[at_blocks[i], :]) for i in range(4))
        grad = sum(dot00(w[i][:, 2 * 128 :], cot[at_blocks[i], :]) for i in range(4))
        cosine, sine = tables[2 * u], tables[2 * u + 1]
        for h in range(heads):
            dims = slice(u * sub, (u + 1) * sub)
            at = h * sub
            q_ref[h, dims, :] = turn(pre[at : at + sub], cosine, sine).astype(bf16)
            at += third
            kv_ref[0, h, dims, :] = turn(pre[at : at + sub], cosine, sine).astype(bf16)
            at += third
            kv_ref[1, h, dims, :] = pre[at : at + sub].astype(bf16)
            at += third - 2 * 128
            ga_ref[h, dims, :] = grad[at : at + sub].astype(bf16)


def put_sums(refs, i, u, value):
    own, keep, give, far = refs
    half = value.shape[1]
    side = 1 - u if i == 2 else u
    (own, keep, give, far)[i][:, side * half : (side + 1) * half] = value.astype(own.dtype if i == 0 else bf16)


def rows_at(first, *rows):
    at = lax.broadcasted_iota(jnp.int32, (PAD, rows[0].shape[1]), 0)
    return sum(jnp.where(at == first + i, row, 0.0) for i, row in enumerate(rows))


def add_below(ref, rows):
    size = rows.shape[1]
    ref[-PAD:, :size] = (ref[-PAD:, :size].astype(f32) + rows).astype(ref.dtype)


def swapped(x):
    sub = HD // 2
    return jnp.concatenate([x[sub:], x[:sub]], axis=0)


def attention_kernel(
    span, scal, start, q_ref, kv_ref, k_other, v_other, ga_ref, att_ref, gq_ref, gkv_ref, gkv_other, kc, vc, gk, gv
):
    count = q_ref.shape[2]
    rows = 2 * count // span
    half = span // 2
    core = scal[1]
    for rr in range(rows):
        mine, lanes = slice(rr * half, (rr + 1) * half), rr * span
        for at, ref, other in ((0, kc, k_other), (1, vc, v_other)):
            ref[:, lanes : lanes + half] = kv_ref[at, 0, :, mine]
            ref[:, lanes + half : lanes + span] = swapped(other[0, 0, :, mine])
    kt, vt = kc[...].T, vc[...].T
    gk[...] = jnp.zeros_like(gk)
    gv[...] = jnp.zeros_like(gv)
    scale = HD ** (-0.5)
    for a in range(rows):
        size = (a + 1) * span
        mine = slice(a * half, (a + 1) * half)
        q, ga = q_ref[0, :, mine], ga_ref[0, :, mine]
        key = lax.broadcasted_iota(jnp.int32, (size, 1), 0)
        at = key % span
        key = key - at + jnp.where((at >= half) == (core == 0), half, 0) + at % half
        query = lax.broadcasted_iota(jnp.int32, (1, half), 1) + (a * span + core * half)
        first = start[:, mine]
        allowed = (key <= query) & (key >= first)
        scores = jnp.where(allowed, dot10(kt[:size], q) * scale, -1000000000.0)
        top = jnp.max(scores, axis=0, keepdims=True)
        exponent = jnp.exp(scores - top)
        probs = exponent * (1.0 / jnp.sum(exponent, axis=0, keepdims=True))
        low = probs.astype(bf16)
        att_ref[0, :, mine] = dot10(vc[:, :size], low).astype(bf16)
        grad = dot10(vt[:size], ga)
        total = jnp.sum(grad * probs, axis=0, keepdims=True)
        grad = (probs * (grad - total) * scale).astype(bf16)
        gq_ref[0, :, mine] = dot10(kc[:, :size], grad)
        gk[:, :size] += dot11(q, grad)
        gv[:, :size] += dot11(ga, low)
    for rr in range(rows):
        mine, lanes = slice(rr * half, (rr + 1) * half), rr * span
        for ref, at in ((gk, 0), (gv, 1)):
            gkv_ref[at, 0, :, mine] = ref[:, lanes : lanes + half]
            gkv_other[at, 0, :, mine] = ref[:, lanes + half : lanes + span].astype(bf16)


def qkv_grad_kernel(heads, scal, tables, gq_ref, gkv_ref, gk_other, gv_other, att_ref, xn, cot, *refs):
    sub = HD // 2
    third = heads * sub
    outs, sums = refs[:4], refs[4:]
    at_blocks = blocks_of(scal[1], sums[0].shape[0])
    zeros = jnp.zeros((third, xn.shape[1]), bf16)
    for u in range(2):
        grads_ref, att_out = outs[2 * u : 2 * u + 2]
        cosine, sine = tables[2 * u], tables[2 * u + 1]
        dims = slice(u * sub, (u + 1) * sub)
        swap = slice((1 - u) * sub, (2 - u) * sub)
        for h in range(heads):
            at = h * sub
            grads_ref[at : at + sub, :] = turn(gq_ref[h, dims, :], cosine, -sine).astype(bf16)
            g = gkv_ref[0, h, dims, :] + gk_other[0, h, swap, :].astype(f32)
            at += third
            grads_ref[at : at + sub, :] = turn(g, cosine, -sine).astype(bf16)
            g = gkv_ref[1, h, dims, :] + gv_other[0, h, swap, :].astype(f32)
            at += third
            grads_ref[at : at + sub, :] = g.astype(bf16)
            at += third
            att_out[at : at + sub, :] = att_ref[h, dims, :]
        grads_ref[3 * third :, :] = zeros
        for s in range(3):
            att_out[s * third : (s + 1) * third, :] = zeros
        for i in range(4):
            total = dot11(xn[at_blocks[i], :], grads_ref[...]) + dot11(cot[at_blocks[i], :], att_out[...])
            put_sums(sums, i, u, total)


def feed_kernel(scal, xn, cot, *refs):
    weights, acts, sums = refs[:4], refs[4:8], refs[8:]
    at_blocks = blocks_of(scal[1], weights[0].shape[0])
    part = acts[0].shape[0]
    for u in range(2):
        up_ref, grad_ref = acts[2 * u : 2 * u + 2]
        w = [weight(weights, i, u) for i in range(4)]
        pre = sum(dot00(w[i][:, :part], xn[at_blocks[i], :]) for i in range(4))
        phi = 0.5 * (1.0 + lax.erf(pre * (0.5**0.5)))
        slope = phi + pre * (jnp.exp(-0.5 * pre * pre) * 0.3989422804014327)
        up_ref[...] = (pre * phi).astype(bf16)
        grad = sum(dot00(w[i][:, part:], cot[at_blocks[i], :]) for i in range(4))
        grad_ref[...] = (grad * slope).astype(bf16)
        for i in range(4):
            total = [dot11(xn[at_blocks[i], :], grad_ref[...]), dot11(cot[at_blocks[i], :], up_ref[...])]
            put_sums(sums, i, u, jnp.concatenate(total, axis=1))


def back_kernel(scal, *refs):
    w1, w2, acts, outs = refs[:4], refs[4:8], refs[8:16], refs[16:]
    part = acts[4].shape[0]
    rows, (_, _, width, span) = len(outs), outs[0].shape
    row, core = scal[0], scal[1]
    for i, to in enumerate((0, 3 - core, 2 + core, 1)):
        for way in range(2):
            side = slice((1 - way) * part, (2 - way) * part)
            total = sum(dot10(weight(w1, i, u), acts[2 * way + u][...]) for u in range(2))
            total += sum(dot10(weight(w2, i, u)[:, side], acts[4 + 2 * way + u][...]) for u in range(2))
            total = total[:width].astype(bf16)
            for j, out in enumerate(outs):
                value = total[:, :span]
                for rr in range(1, rows):
                    value = jnp.where((row ^ j) == rr, total[:, rr * span : (rr + 1) * span], value)
                out[to, way] = value


def pair_kernel(keep, *refs):
    near, size = refs[-1], refs[0].shape[1]
    for j, got in enumerate(refs[:-1]):
        cols = slice(j * size, (j + 1) * size)
        near[:, cols] = (keep[:, cols].astype(f32) + got[...].astype(f32)).astype(bf16)


def total_kernel(near1, far1, own1, near2, far2, own2, c_sum, out):
    at = own1.shape[1]
    out[:, :at] = (near1[...].astype(f32) + far1[...].astype(f32) + own1[...]).astype(bf16)
    out[:, at:] = (near2[...].astype(f32) + far2[...].astype(f32) + own2[...]).astype(bf16)
    add_below(out, rows_at(4, c_sum[...]))


def halves_of(here, there, at, size):
    def theirs(cols):
        piece = there[cols // there[0].shape[1]]
        cols = cols % there[0].shape[1]
        return piece[:, cols : cols + size].astype(f32)

    mine = here[:, at : at + size].astype(f32) + theirs(at + size)
    return mine, here[:, at + size : at + 2 * size].astype(f32) + theirs(at)


def small_kernel(here, there0, there1, there2, own1, own2, out):
    there = (there0, there1, there2)
    width = out.shape[1]
    rows, at = [], 0
    for own, used in ((own1, 3 * own1.shape[1] // 8), (own2, own2.shape[1] // 4)):
        half = own.shape[1] // 2
        gain = bias = 0.0
        for u, m in enumerate(halves_of(here, there, at, half)):
            w = own[:width, u * half : u * half + used]
            ones = jnp.ones((8, used), bf16)
            gain += dot11(ones, (m[:width, :used] * w.astype(f32)).astype(bf16))
            bias += dot11(jnp.broadcast_to(m[width : width + 1, :used], ones.shape).astype(bf16), w)
        rows += [gain[:1], bias[:1]]
        at += 2 * half
    cols = slice(0, width)
    rows.append(here[width:, cols].astype(f32)[4:5] + there0[width:, cols].astype(f32)[4:5])
    out[...] = jnp.concatenate(rows + [jnp.zeros((3, width), f32)], axis=0)


def final_kernel(scal, here, there0, there1, there2, scales, d_wq, d_wd, d_win, d_wout, d_bq, d_bf):
    there = (there0, there1, there2)
    heads, width, _ = d_wd.shape
    sub = HD // 2
    tail = d_win.shape[1]
    part = tail // 2
    third = heads * sub
    core = scal[1]
    at = lax.broadcasted_iota(jnp.int32, (8, 128), 0)
    eye = (at == lax.broadcasted_iota(jnp.int32, (8, 128), 1)).astype(f32).astype(bf16)
    columns = dot00(scales[...], eye)
    gain1, shift1, gain2, shift2 = (columns[:, i : i + 1] for i in range(4))

    def in_order(pair):
        mine, theirs = pair
        return jnp.where(core == 0, mine, theirs), jnp.where(core == 0, theirs, mine)

    for a, m in enumerate(in_order(halves_of(here, there, 0, 4 * third))):
        dims = slice(a * sub, (a + 1) * sub)
        row = m[width : width + 1, : 3 * third]
        grad = m[:width, : 3 * third] * gain1 + shift1 * row
        for s in range(3):
            for h in range(heads):
                at = (s * heads + h) * sub
                d_wq[s, h, :, dims] = grad[:, at : at + sub]
                d_bq[s : s + 1, h * HD + a * sub : h * HD + (a + 1) * sub] = row[:, at : at + sub]
        for h in range(heads):
            at = 3 * third + h * sub
            d_wd[h, :, dims] = m[:width, at : at + sub]
    for a, m in enumerate(in_order(halves_of(here, there, 8 * third, tail))):
        cols = slice(a * part, (a + 1) * part)
        row = m[width : width + 1, :part]
        d_bf[:, cols] = row
        d_win[:, cols] = m[:width, :part] * gain2 + shift2 * row
        d_wout[:, cols] = m[:width, part:]


def row_kernel(scal, x_ref, *refs):
    parts, outs = refs[:4], refs[4:]
    crossed = scal[2]
    x = x_ref[:, 0].astype(f32)
    x = x - jnp.mean(x, axis=(0, 1), keepdims=True)
    rstd = lax.rsqrt(jnp.mean(x * x, axis=(0, 1), keepdims=True) + EPS)
    x = x * rstd
    sums = []
    for way in range(2):
        total = sum(p[:, way].astype(f32) for p in parts)
        sums.append([jnp.where(crossed == 1, total[k ^ 2], total[k]) for k in range(4)])
    grad = jnp.stack(sums[1])
    grad = rstd * (
        grad
        - jnp.mean(grad, axis=(0, 1), keepdims=True)
        - x * jnp.mean(grad * x, axis=(0, 1), keepdims=True)
    )
    for k in range(4):
        outs[k][0] = sums[0][k].astype(bf16)
        outs[k][1] = grad[k].astype(bf16)


def body(
    hidden_in,
    segments,
    w_qkv,
    b_qkv,
    w_dense,
    b_dense,
    ln1_gain,
    ln1_bias,
    ln2_gain,
    ln2_bias,
    w_in,
    b_in,
    w_out,
    b_out,
    cotangent,
):
    width, seqs, span = hidden_in.shape
    half_span = span // 2
    cols, rows, dps = lax.axis_size("col"), lax.axis_size("row"), lax.axis_size("dp")
    heads = w_qkv.shape[1]
    hw = heads * HD
    sub = HD // 2
    ff = w_in.shape[1]
    core = lax.axis_index("dp") % 2
    row = lax.axis_index("row")
    col = lax.axis_index("col")
    first_core = core == 0
    crossed = (core ^ (col >> 1)) == 1
    block = width + PAD
    count = rows * half_span

    counts = jnp.stack([jnp.sum(segments < 1, axis=1), jnp.sum(segments < 2, axis=1)], axis=1)
    counts = jnp.stack([counts // 256, counts % 256], axis=2).reshape(seqs, 4).astype(bf16)
    counts = jnp.pad(counts[:, None], ((0, 0), (0, PAD - 1), (0, half_span - 4)))
    pieces = []
    for j in range(4):
        at, where = j % 2, slice((j // 2) * half_span, (j // 2 + 1) * half_span)
        pieces.append(jnp.concatenate([hidden_in[:, at, where], cotangent[:, at, where], counts[at]]))
    sent = swap_by(col, pieces)
    got = [lax.ppermute(sent[k], ("dp", "col"), spread_peers(k)) for k in range(4)]
    counts = got[0][2 * width, :4].astype(jnp.int32)
    counts = [256 * counts[0] + counts[1], 256 * counts[2] + counts[3]]
    mine = jnp.stack([g[: 2 * width].reshape(2, width, half_span) for g in got])
    tokens = gather_xor(mine, "row")

    scalars = jnp.stack([row, core, crossed.astype(jnp.int32)])

    gain1, shift1 = ln1_gain.astype(f32), ln1_bias.astype(f32)
    gain2, shift2 = ln2_gain.astype(f32), ln2_bias.astype(f32)

    def in_order(halves):
        low, high = halves
        return jnp.concatenate([pick(first_core, low, high), pick(first_core, high, low)], axis=-1)

    wq = w_qkv.reshape(3, heads, width, 2, sub).transpose(3, 2, 0, 1, 4).reshape(2, width, -1)
    wd = w_dense.reshape(heads, width, 2, sub).transpose(2, 1, 0, 3).reshape(2, width, -1)
    bias_q = b_qkv.reshape(3, heads, 2, sub).transpose(2, 0, 1, 3).reshape(2, -1).astype(f32) / cols
    part = ff // 2
    bias_f = b_in.reshape(2, part).astype(f32) / cols
    halves1, halves2 = [], []
    for u in range(2):
        w = wq[u].astype(f32)
        bias = jnp.sum(w * shift1[:, None], axis=0) + bias_q[u]
        halves1.append(
            extend(
                jnp.concatenate([w * gain1[:, None], wd[u].astype(f32)], axis=1),
                jnp.concatenate([bias, jnp.zeros((heads * sub,), f32)]),
            )
        )
        w = w_in[:, u * part : (u + 1) * part].astype(f32)
        bias = jnp.sum(w * shift2[:, None], axis=0) + bias_f[u]
        halves2.append(
            extend(
                jnp.concatenate([w * gain2[:, None], w_out[:, u * part : (u + 1) * part].astype(f32)], axis=1),
                jnp.concatenate([bias, jnp.zeros((part,), f32)]),
            )
        )

    head, tail = 2 * hw, 2 * part
    own1, own2 = in_order(halves1), in_order(halves2)
    own1 = after(own1, got[:2])
    near1, far1 = send_near(own1), send(own1, "col", 1)
    near2 = send_near(after(own2, [near1]))
    w1 = [own1, near1, send(near1, "dp", 1), far1]
    far2 = send(after(own2, [far1, w1[2]]), "col", 1)

    base = jnp.arange(half_span, dtype=jnp.int32)
    q_pos = jnp.concatenate([rr * span + core * half_span + base for rr in range(rows)])
    q_start = jnp.where(q_pos >= counts[1], counts[1], jnp.where(q_pos >= counts[0], counts[0], 0))
    frequency = 10000.0 ** (-jnp.arange(ROT // 2, dtype=f32) * 2.0 / ROT)
    angles = (q_pos - q_start).astype(f32)[None, :] * frequency[:, None]
    cosine, sine = jnp.cos(angles), jnp.sin(angles)
    unit, nil = jnp.ones_like(cosine), jnp.zeros_like(sine)
    tables = jnp.stack(
        [
            pick(first_core, cosine, unit),
            pick(first_core, sine, nil),
            pick(first_core, unit, cosine),
            pick(first_core, nil, sine),
        ]
    )

    grid_shape = (cols * block, count)
    xn, cot = call(place_kernel, [shaped(grid_shape, bf16)] * 2, tokens, scalars)
    queries, kv, grad_att = call(
        partial(qkv_kernel, heads),
        [
            shaped((heads, HD, count), bf16),
            shaped((2, heads, HD, count), bf16),
            shaped((heads, HD, count), bf16),
        ],
        [tables, xn, cot, *w1],
        scalars,
    )
    kv_other = [send(kv[:1], "dp", 1), send(kv[1:], "dp", 1)]

    by_head = pl.BlockSpec((1, HD, count), lambda h: (h, 0, 0))
    by_head1 = pl.BlockSpec((1, 1, HD, count), lambda h: (0, h, 0, 0))
    by_head2 = pl.BlockSpec((2, 1, HD, count), lambda h: (0, h, 0, 0))
    attended, grad_q, grad_kv, grad_kv_other = pl.pallas_call(
        partial(attention_kernel, span),
        grid=(heads,),
        in_specs=[
            pl.BlockSpec(memory_space=pltpu.SMEM),
            pl.BlockSpec((1, count), lambda h: (0, 0)),
            by_head,
            by_head2,
            by_head1,
            by_head1,
            by_head,
        ],
        out_specs=[by_head, by_head, by_head2, by_head2],
        out_shape=[
            shaped((heads, HD, count), bf16),
            shaped((heads, HD, count), f32),
            shaped((2, heads, HD, count), f32),
            shaped((2, heads, HD, count), bf16),
        ],
        scratch_shapes=[
            pltpu.VMEM((HD, 2 * count), bf16),
            pltpu.VMEM((HD, 2 * count), bf16),
            pltpu.VMEM((HD, 2 * count), f32),
            pltpu.VMEM((HD, 2 * count), f32),
        ],
        compiler_params=pltpu.CompilerParams(vmem_limit_bytes=48 * 2**20),
        cost_estimate=pl.CostEstimate(
            flops=0, bytes_accessed=0, transcendentals=0
        ),
    )(scalars, q_start[None, :], queries, kv, *kv_other, grad_att)
    grad_kv_got = [send(grad_kv_other[:1], "dp", 1), send(grad_kv_other[1:], "dp", 1)]

    def sums(size):
        return [shaped((block, size), f32)] + [shaped((block, size), bf16)] * 3

    half_act = shaped((head, count), bf16)
    grads_a, att_a, grads_b, att_b, sum1, keep1, give1, far_sum1 = call(
        partial(qkv_grad_kernel, heads),
        [half_act] * 4 + sums(2 * head),
        [tables, grad_q, grad_kv, *grad_kv_got, attended, xn, cot],
        scalars,
    )
    got1 = send(give1, "dp", 1)
    low_near1 = call(pair_kernel, [shaped((block, 2 * head), bf16)], [keep1, got1])[0]
    sum_near1 = send_near(low_near1)
    sum_far1 = send(far_sum1, "col", 1)

    near2, far2 = after([near2, far2], [keep1])
    near2 = after(near2, [far2])
    w2 = [own2, near2, send(near2, "dp", 1), far2]
    act = shaped((part, count), bf16)
    up_a, hid_a, up_b, hid_b, sum2, keep2, give2, far_sum2 = call(
        feed_kernel, [act] * 4 + sums(2 * tail), [after(xn, low_near1), cot, *w2], scalars
    )
    third = 2 * tail // 3
    got2 = [send(give2[:, j * third : (j + 1) * third], "dp", 1) for j in range(3)]
    low_near2 = call(pair_kernel, [shaped((block, 2 * tail), bf16)], [keep2, *got2])[0]
    low_near2, far_sum2 = after([low_near2, far_sum2], [sum_near1, sum_far1])
    sum_near2 = send_near(low_near2)
    sum_far2 = send(far_sum2, "col", 1)

    strip = shaped((cols, 2, width, half_span), bf16)
    sums = call(
        back_kernel,
        [strip] * rows,
        [*w1, *w2, att_a, att_b, grads_a, grads_b, up_a, up_b, hid_a, hid_b],
        scalars,
    )
    sums = after(sums, [sum_near1, sum_far1])
    sums = [sums[0]] + [send(sums[j], "row", j) for j in range(1, rows)]
    piece = shaped((2, width, half_span), bf16)
    back = call(row_kernel, [piece] * cols, [mine, *sums], scalars)
    back = after(back, [sum_near2, sum_far2])
    back = [lax.ppermute(back[k], ("dp", "col"), spread_peers(k, True)) for k in range(4)]
    c_sum = jnp.sum(cotangent.astype(f32), axis=(1, 2))[None]
    total = call(
        total_kernel,
        [shaped((block, 2 * (head + tail)), bf16)],
        [sum_near1, sum_far1, sum1, sum_near2, sum_far2, sum2, c_sum],
    )[0]
    wide = total.astype(f32)
    for k in range(2, dps, 2):
        wide = wide + lax.ppermute(total, "dp", turn_peers(k)).astype(f32)
    total = wide.astype(bf16)
    third = (head + tail) * 2 // 3
    other = [send(total[:, j * third : (j + 1) * third], "dp", 1) for j in range(3)]
    small = call(small_kernel, [shaped((8, width), f32)], [total, *other, own1, own2])[0]
    small = small + send(small, "row", 1)
    small = small + send(small, "row", 2)
    scales = jnp.pad(jnp.stack([ln1_gain, ln1_bias, ln2_gain, ln2_bias]), ((0, 4), (0, 0)))
    d_wq, d_wd, d_w_in, d_w_out, d_bq, d_bf = call(
        final_kernel,
        [
            shaped((3, heads, width, HD), f32),
            shaped((heads, width, HD), f32),
            shaped((width, ff), f32),
            shaped((width, ff), f32),
            shaped((3, hw), f32),
            shaped((1, ff), f32),
        ],
        [total, *other, scales],
        scalars,
    )
    back = after(back, d_bf)
    back = swap_by(col, back)
    branch, grad_x = jnp.stack(
        [jnp.concatenate([back[s], back[2 + s]], axis=2) for s in range(2)], axis=2
    ).astype(f32)
    bias_out = b_dense.astype(f32) + b_out.astype(f32)
    layer_out = (hidden_in.astype(f32) + branch + bias_out[:, None, None]).astype(bf16)
    grad_in = cotangent.astype(f32) + grad_x

    return (
        layer_out,
        grad_in,
        d_wq.reshape(w_qkv.shape),
        d_bq,
        d_wd.reshape(w_dense.shape),
        small[4],
        small[0] / gain1,
        small[1] / gain1,
        small[2] / gain2,
        small[3] / gain2,
        d_w_in,
        d_bf.reshape(ff),
        d_w_out,
        small[4],
    )


def solution(mesh):
    placed = (
        P("col", "dp", "row"),
        P("dp", None),
        P(None, "row", "col"),
        P(None, "row"),
        P("row", "col"),
        P("col"),
        P("col"),
        P("col"),
        P("col"),
        P("col"),
        P("col", "row"),
        P("row"),
        P("col", "row"),
        P("col"),
        P("col", "dp", "row"),
    )
    return jax.shard_map(
        body,
        mesh=mesh,
        in_specs=placed,
        out_specs=(
            P("col", "dp", "row"),
            P("col", "dp", "row"),
            P(None, "row", "col"),
            P(None, "row"),
            P("row", "col"),
            P("col"),
            P("col"),
            P("col"),
            P("col"),
            P("col"),
            P("col", "row"),
            P("row"),
            P("col", "row"),
            P("col"),
        ),
        check_vma=False,
    )
```

```python
from functools import partial

import jax
import jax.numpy as jnp
from jax import lax
from jax.experimental import pallas as pl
from jax.experimental.pallas import tpu as pltpu
from jax.sharding import PartitionSpec as P

D = 768
HD = 64
ROT = 16
EPS = 1e-05
PAD = 16

f32 = jnp.float32
bf16 = jnp.bfloat16


def xor_peers(axis, shift):
    return [(i, i ^ shift) for i in range(lax.axis_size(axis))]


def turn_peers(shift):
    count = lax.axis_size("dp")
    return [(i, (i + shift) % count) for i in range(count)]


def send(x, axis, shift):
    return lax.ppermute(x, axis, xor_peers(axis, shift))


def send_near(x):
    pairs = []
    cols = lax.axis_size("col")
    for dp in range(lax.axis_size("dp")):
        pairs += [(dp * cols + c, dp * cols + (c ^ (3 - dp % 2))) for c in range(cols)]
    return lax.ppermute(x, ("dp", "col"), pairs)


def gather_xor(x, axis):
    return [x] + [send(x, axis, k) for k in range(1, lax.axis_size(axis))]


def after(x, others):
    return lax.optimization_barrier((x, others))[0]


def spread_peers(round_of, back=False):
    pairs = []
    cols = lax.axis_size("col")
    for dp in range(lax.axis_size("dp")):
        for col in range(cols):
            half, seq = divmod(col ^ round_of, 2)
            target = (dp // 2 * 2 + half) * cols + 2 * (dp % 2) + seq
            pairs.append((dp * cols + col, target))
    return [(b, a) for a, b in pairs] if back else pairs


def pick(flag, first, second):
    return jnp.where(flag, first, second)


def swap_by(code, parts):
    parts = [pick((code & 1) == 1, parts[j ^ 1], parts[j]) for j in range(4)]
    return [pick((code & 2) == 2, parts[j ^ 2], parts[j]) for j in range(4)]


def sum_parts(parts):
    total = parts[0].astype(f32)
    for part in parts[1:]:
        total = total + part.astype(f32)
    return total


def dot(a, b, contract):
    return lax.dot_general(a, b, (contract, ((), ())), preferred_element_type=f32)


def extend(columns, bias):
    high = lax.reduce_precision(bias, 8, 7)
    rows = jnp.stack([high, bias - high]).astype(bf16)
    rows = jnp.pad(rows, ((0, PAD - 2), (0, 0)))
    return jnp.concatenate([columns.astype(bf16), rows], axis=0)


def call(kernel, outs, args, scalars=None, cost=0):
    specs = [pl.BlockSpec(memory_space=pltpu.VMEM) for _ in args]
    if scalars is not None:
        specs = [pl.BlockSpec(memory_space=pltpu.SMEM)] + specs
        args = [scalars, *args]
    return pl.pallas_call(
        kernel,
        out_shape=outs,
        in_specs=specs,
        out_specs=[pl.BlockSpec(memory_space=pltpu.VMEM) for _ in outs],
        compiler_params=pltpu.CompilerParams(vmem_limit_bytes=48 * 2**20),
        cost_estimate=pl.CostEstimate(flops=cost, bytes_accessed=0, transcendentals=0),
    )(*args)


def shaped(shape, dtype):
    return jax.ShapeDtypeStruct(shape, dtype)


def place_kernel(scal, *refs):
    parts, (xn_ref, cot_ref) = refs[:4], refs[4:]
    block = xn_ref.shape[0] // 4
    width, span = parts[0].shape[2:]
    row, crossed = scal[0], scal[2]
    for j in range(4):
        ref = parts[j]
        at = pl.multiple_of((row ^ j) * span, span)
        x = ref[:, 0].astype(f32)
        x = x - jnp.mean(x, axis=(0, 1), keepdims=True)
        x = (x * lax.rsqrt(jnp.mean(x * x, axis=(0, 1), keepdims=True) + EPS)).astype(bf16)
        for k in range(4):
            to = pl.multiple_of((k ^ (2 * crossed)) * block, PAD)
            xn_ref[pl.ds(to, width), pl.ds(at, span)] = x[k]
            cot_ref[pl.ds(to, width), pl.ds(at, span)] = ref[k, 1]
    rest = (lax.broadcasted_iota(jnp.int32, (PAD, xn_ref.shape[1]), 0) < 2).astype(f32).astype(bf16)
    for k in range(4):
        xn_ref[k * block + width : (k + 1) * block, :] = rest
        cot_ref[k * block + width : (k + 1) * block, :] = jnp.zeros_like(rest)


def turn(x, cosine, sine):
    half = ROT // 2
    a, b = x[:half], x[half:ROT]
    return jnp.concatenate([a * cosine - b * sine, b * cosine + a * sine, x[ROT:]], axis=0)


def dot00(a, b):
    return dot(a, b, ((0,), (0,)))


def dot11(a, b):
    return dot(a, b, ((1,), (1,)))


def dot10(a, b):
    return dot(a, b, ((1,), (0,)))


def weight(parts, i, u):
    half = parts[i].shape[1] // 2
    side = 1 - u if i == 2 else u
    return parts[i][:, side * half : (side + 1) * half]


def blocks_of(core, size):
    return [pl.ds(pl.multiple_of(b * size, PAD), size) for b in (0, 3 - core, 2 + core, 1)]


def qkv_kernel(heads, scal, tables, xn, cot, *refs):
    weights, (q_ref, kv_ref, ga_ref) = refs[:4], refs[4:]
    sub = HD // 2
    at_blocks = blocks_of(scal[1], weights[0].shape[0])
    third = heads * sub
    for u in range(2):
        w = [weight(weights, i, u) for i in range(4)]
        pre = sum(dot00(w[i], xn[at_blocks[i], :]) for i in range(4))
        grad = sum(dot00(w[i][:, 2 * 128 :], cot[at_blocks[i], :]) for i in range(4))
        cosine, sine = tables[2 * u], tables[2 * u + 1]
        for h in range(heads):
            dims = slice(u * sub, (u + 1) * sub)
            at = h * sub
            q_ref[h, dims, :] = turn(pre[at : at + sub], cosine, sine).astype(bf16)
            at += third
            kv_ref[0, h, dims, :] = turn(pre[at : at + sub], cosine, sine).astype(bf16)
            at += third
            kv_ref[1, h, dims, :] = pre[at : at + sub].astype(bf16)
            at += third - 2 * 128
            ga_ref[h, dims, :] = grad[at : at + sub].astype(bf16)


def put_sums(refs, i, u, value):
    own, keep, give, far = refs
    half = value.shape[1]
    side = 1 - u if i == 2 else u
    (own, keep, give, far)[i][:, side * half : (side + 1) * half] = value.astype(own.dtype if i == 0 else bf16)


def rows_at(first, *rows):
    at = lax.broadcasted_iota(jnp.int32, (PAD, rows[0].shape[1]), 0)
    return sum(jnp.where(at == first + i, row, 0.0) for i, row in enumerate(rows))


def add_below(ref, rows):
    size = rows.shape[1]
    ref[-PAD:, :size] = (ref[-PAD:, :size].astype(f32) + rows).astype(ref.dtype)


def swapped(x):
    sub = HD // 2
    return jnp.concatenate([x[sub:], x[:sub]], axis=0)


def attention_kernel(
    span, scal, start, q_ref, kv_ref, k_other, v_other, ga_ref, att_ref, gq_ref, gkv_ref, gkv_other, kc, vc, gk, gv
):
    count = q_ref.shape[2]
    rows = 2 * count // span
    half = span // 2
    core = scal[1]
    for rr in range(rows):
        mine, lanes = slice(rr * half, (rr + 1) * half), rr * span
        for at, ref, other in ((0, kc, k_other), (1, vc, v_other)):
            ref[:, lanes : lanes + half] = kv_ref[at, 0, :, mine]
            ref[:, lanes + half : lanes + span] = swapped(other[0, 0, :, mine])
    kt, vt = kc[...].T, vc[...].T
    gk[...] = jnp.zeros_like(gk)
    gv[...] = jnp.zeros_like(gv)
    scale = HD ** (-0.5)
    for a in range(rows):
        size = (a + 1) * span
        mine = slice(a * half, (a + 1) * half)
        q, ga = q_ref[0, :, mine], ga_ref[0, :, mine]
        key = lax.broadcasted_iota(jnp.int32, (size, 1), 0)
        at = key % span
        key = key - at + jnp.where((at >= half) == (core == 0), half, 0) + at % half
        query = lax.broadcasted_iota(jnp.int32, (1, half), 1) + (a * span + core * half)
        first = start[:, mine]
        allowed = (key <= query) & (key >= first)
        scores = jnp.where(allowed, dot10(kt[:size], q) * scale, -1000000000.0)
        top = jnp.max(scores, axis=0, keepdims=True)
        exponent = jnp.exp(scores - top)
        probs = exponent * (1.0 / jnp.sum(exponent, axis=0, keepdims=True))
        low = probs.astype(bf16)
        att_ref[0, :, mine] = dot10(vc[:, :size], low).astype(bf16)
        grad = dot10(vt[:size], ga)
        total = jnp.sum(grad * probs, axis=0, keepdims=True)
        grad = (probs * (grad - total) * scale).astype(bf16)
        gq_ref[0, :, mine] = dot10(kc[:, :size], grad)
        gk[:, :size] += dot11(q, grad)
        gv[:, :size] += dot11(ga, low)
    for rr in range(rows):
        mine, lanes = slice(rr * half, (rr + 1) * half), rr * span
        for ref, at in ((gk, 0), (gv, 1)):
            gkv_ref[at, 0, :, mine] = ref[:, lanes : lanes + half]
            gkv_other[at, 0, :, mine] = ref[:, lanes + half : lanes + span].astype(bf16)


def qkv_grad_kernel(heads, scal, tables, gq_ref, gkv_ref, gk_other, gv_other, att_ref, xn, cot, *refs):
    sub = HD // 2
    third = heads * sub
    outs, sums = refs[:4], refs[4:]
    at_blocks = blocks_of(scal[1], sums[0].shape[0])
    zeros = jnp.zeros((third, xn.shape[1]), bf16)
    for u in range(2):
        grads_ref, att_out = outs[2 * u : 2 * u + 2]
        cosine, sine = tables[2 * u], tables[2 * u + 1]
        dims = slice(u * sub, (u + 1) * sub)
        swap = slice((1 - u) * sub, (2 - u) * sub)
        for h in range(heads):
            at = h * sub
            grads_ref[at : at + sub, :] = turn(gq_ref[h, dims, :], cosine, -sine).astype(bf16)
            g = gkv_ref[0, h, dims, :] + gk_other[0, h, swap, :].astype(f32)
            at += third
            grads_ref[at : at + sub, :] = turn(g, cosine, -sine).astype(bf16)
            g = gkv_ref[1, h, dims, :] + gv_other[0, h, swap, :].astype(f32)
            at += third
            grads_ref[at : at + sub, :] = g.astype(bf16)
            at += third
            att_out[at : at + sub, :] = att_ref[h, dims, :]
        grads_ref[3 * third :, :] = zeros
        for s in range(3):
            att_out[s * third : (s + 1) * third, :] = zeros
        for i in range(4):
            total = dot11(xn[at_blocks[i], :], grads_ref[...]) + dot11(cot[at_blocks[i], :], att_out[...])
            put_sums(sums, i, u, total)


def feed_kernel(scal, xn, cot, *refs):
    weights, acts, sums = refs[:4], refs[4:8], refs[8:]
    at_blocks = blocks_of(scal[1], weights[0].shape[0])
    part = acts[0].shape[0]
    for u in range(2):
        up_ref, grad_ref = acts[2 * u : 2 * u + 2]
        w = [weight(weights, i, u) for i in range(4)]
        pre = sum(dot00(w[i][:, :part], xn[at_blocks[i], :]) for i in range(4))
        phi = 0.5 * (1.0 + lax.erf(pre * (0.5**0.5)))
        slope = phi + pre * (jnp.exp(-0.5 * pre * pre) * 0.3989422804014327)
        up_ref[...] = (pre * phi).astype(bf16)
        grad = sum(dot00(w[i][:, part:], cot[at_blocks[i], :]) for i in range(4))
        grad_ref[...] = (grad * slope).astype(bf16)
        for i in range(4):
            total = [dot11(xn[at_blocks[i], :], grad_ref[...]), dot11(cot[at_blocks[i], :], up_ref[...])]
            put_sums(sums, i, u, jnp.concatenate(total, axis=1))


def back_kernel(scal, *refs):
    w1, w2, acts, outs = refs[:4], refs[4:8], refs[8:16], refs[16:]
    part = acts[4].shape[0]
    rows, (_, _, width, span) = len(outs), outs[0].shape
    row, core = scal[0], scal[1]
    for i, to in enumerate((0, 3 - core, 2 + core, 1)):
        for way in range(2):
            side = slice((1 - way) * part, (2 - way) * part)
            total = sum(dot10(weight(w1, i, u), acts[2 * way + u][...]) for u in range(2))
            total += sum(dot10(weight(w2, i, u)[:, side], acts[4 + 2 * way + u][...]) for u in range(2))
            total = total[:width].astype(bf16)
            for j, out in enumerate(outs):
                value = total[:, :span]
                for rr in range(1, rows):
                    value = jnp.where((row ^ j) == rr, total[:, rr * span : (rr + 1) * span], value)
                out[to, way] = value


def pair_kernel(keep, *refs):
    near, size = refs[-1], refs[0].shape[1]
    for j, got in enumerate(refs[:-1]):
        cols = slice(j * size, (j + 1) * size)
        near[:, cols] = (keep[:, cols].astype(f32) + got[...].astype(f32)).astype(bf16)


def total_kernel(near1, far1, own1, near2, far2, own2, c_sum, out):
    at = own1.shape[1]
    out[:, :at] = (near1[...].astype(f32) + far1[...].astype(f32) + own1[...]).astype(bf16)
    out[:, at:] = (near2[...].astype(f32) + far2[...].astype(f32) + own2[...]).astype(bf16)
    add_below(out, rows_at(4, c_sum[...]))


def halves_of(here, there, at, size):
    def theirs(cols):
        piece = there[cols // there[0].shape[1]]
        cols = cols % there[0].shape[1]
        return piece[:, cols : cols + size].astype(f32)

    mine = here[:, at : at + size].astype(f32) + theirs(at + size)
    return mine, here[:, at + size : at + 2 * size].astype(f32) + theirs(at)


def small_kernel(here, there0, there1, there2, own1, own2, out):
    there = (there0, there1, there2)
    width = out.shape[1]
    rows, at = [], 0
    for own, used in ((own1, 3 * own1.shape[1] // 8), (own2, own2.shape[1] // 4)):
        half = own.shape[1] // 2
        gain = bias = 0.0
        for u, m in enumerate(halves_of(here, there, at, half)):
            w = own[:width, u * half : u * half + used]
            ones = jnp.ones((8, used), bf16)
            gain += dot11(ones, (m[:width, :used] * w.astype(f32)).astype(bf16))
            bias += dot11(jnp.broadcast_to(m[width : width + 1, :used], ones.shape).astype(bf16), w)
        rows += [gain[:1], bias[:1]]
        at += 2 * half
    cols = slice(0, width)
    shared = here[width:, cols].astype(f32)[4:5] + there0[width:, cols].astype(f32)[4:5]
    out[...] = jnp.concatenate(rows + [shared, shared, jnp.zeros((2, width), f32)], axis=0)


def final_kernel(scal, here, there0, there1, there2, scales, d_wq, d_wd, d_win, d_wout, d_bq, d_bf):
    there = (there0, there1, there2)
    heads, width, _ = d_wd.shape
    sub = HD // 2
    tail = d_win.shape[1]
    part = tail // 2
    third = heads * sub
    core = scal[1]
    at = lax.broadcasted_iota(jnp.int32, (8, 128), 0)
    eye = (at == lax.broadcasted_iota(jnp.int32, (8, 128), 1)).astype(f32).astype(bf16)
    columns = dot00(scales[...], eye)
    gain1, shift1, gain2, shift2 = (columns[:, i : i + 1] for i in range(4))

    def in_order(pair):
        mine, theirs = pair
        return jnp.where(core == 0, mine, theirs), jnp.where(core == 0, theirs, mine)

    for a, m in enumerate(in_order(halves_of(here, there, 0, 4 * third))):
        dims = slice(a * sub, (a + 1) * sub)
        row = m[width : width + 1, : 3 * third]
        grad = m[:width, : 3 * third] * gain1 + shift1 * row
        for s in range(3):
            for h in range(heads):
                at = (s * heads + h) * sub
                d_wq[s, h, :, dims] = grad[:, at : at + sub]
                d_bq[s : s + 1, h * HD + a * sub : h * HD + (a + 1) * sub] = row[:, at : at + sub]
        for h in range(heads):
            at = 3 * third + h * sub
            d_wd[h, :, dims] = m[:width, at : at + sub]
    for a, m in enumerate(in_order(halves_of(here, there, 8 * third, tail))):
        cols = slice(a * part, (a + 1) * part)
        row = m[width : width + 1, :part]
        d_bf[:, cols] = row
        d_win[:, cols] = m[:width, :part] * gain2 + shift2 * row
        d_wout[:, cols] = m[:width, part:]


def row_kernel(scal, x_ref, *refs):
    parts, outs = refs[:4], refs[4:]
    crossed = scal[2]
    x = x_ref[:, 0].astype(f32)
    x = x - jnp.mean(x, axis=(0, 1), keepdims=True)
    rstd = lax.rsqrt(jnp.mean(x * x, axis=(0, 1), keepdims=True) + EPS)
    x = x * rstd
    sums = []
    for way in range(2):
        total = sum(p[:, way].astype(f32) for p in parts)
        sums.append([jnp.where(crossed == 1, total[k ^ 2], total[k]) for k in range(4)])
    grad = jnp.stack(sums[1])
    grad = rstd * (
        grad
        - jnp.mean(grad, axis=(0, 1), keepdims=True)
        - x * jnp.mean(grad * x, axis=(0, 1), keepdims=True)
    )
    for k in range(4):
        outs[k][0] = sums[0][k].astype(bf16)
        outs[k][1] = grad[k].astype(bf16)


def body(
    hidden_in,
    segments,
    w_qkv,
    b_qkv,
    w_dense,
    b_dense,
    ln1_gain,
    ln1_bias,
    ln2_gain,
    ln2_bias,
    w_in,
    b_in,
    w_out,
    b_out,
    cotangent,
):
    width, seqs, span = hidden_in.shape
    half_span = span // 2
    cols, rows, dps = lax.axis_size("col"), lax.axis_size("row"), lax.axis_size("dp")
    heads = w_qkv.shape[1]
    hw = heads * HD
    sub = HD // 2
    ff = w_in.shape[1]
    core = lax.axis_index("dp") % 2
    row = lax.axis_index("row")
    col = lax.axis_index("col")
    first_core = core == 0
    crossed = (core ^ (col >> 1)) == 1
    block = width + PAD
    count = rows * half_span

    counts = jnp.stack([jnp.sum(segments < 1, axis=1), jnp.sum(segments < 2, axis=1)], axis=1)
    counts = jnp.stack([counts // 256, counts % 256], axis=2).reshape(seqs, 4).astype(bf16)
    counts = jnp.pad(counts[:, None], ((0, 0), (0, PAD - 1), (0, half_span - 4)))
    pieces = []
    for j in range(4):
        at, where = j % 2, slice((j // 2) * half_span, (j // 2 + 1) * half_span)
        pieces.append(jnp.concatenate([hidden_in[:, at, where], cotangent[:, at, where], counts[at]]))
    sent = swap_by(col, pieces)
    got = [lax.ppermute(sent[k], ("dp", "col"), spread_peers(k)) for k in range(4)]
    counts = got[0][2 * width, :4].astype(jnp.int32)
    counts = [256 * counts[0] + counts[1], 256 * counts[2] + counts[3]]
    mine = jnp.stack([g[: 2 * width].reshape(2, width, half_span) for g in got])
    tokens = gather_xor(mine, "row")

    scalars = jnp.stack([row, core, crossed.astype(jnp.int32)])

    gain1, shift1 = ln1_gain.astype(f32), ln1_bias.astype(f32)
    gain2, shift2 = ln2_gain.astype(f32), ln2_bias.astype(f32)

    def in_order(halves):
        low, high = halves
        return jnp.concatenate([pick(first_core, low, high), pick(first_core, high, low)], axis=-1)

    wq = w_qkv.reshape(3, heads, width, 2, sub).transpose(3, 2, 0, 1, 4).reshape(2, width, -1)
    wd = w_dense.reshape(heads, width, 2, sub).transpose(2, 1, 0, 3).reshape(2, width, -1)
    bias_q = b_qkv.reshape(3, heads, 2, sub).transpose(2, 0, 1, 3).reshape(2, -1).astype(f32) / cols
    part = ff // 2
    bias_f = b_in.reshape(2, part).astype(f32) / cols
    halves1, halves2 = [], []
    for u in range(2):
        w = wq[u].astype(f32)
        bias = jnp.sum(w * shift1[:, None], axis=0) + bias_q[u]
        halves1.append(
            extend(
                jnp.concatenate([w * gain1[:, None], wd[u].astype(f32)], axis=1),
                jnp.concatenate([bias, jnp.zeros((heads * sub,), f32)]),
            )
        )
        w = w_in[:, u * part : (u + 1) * part].astype(f32)
        bias = jnp.sum(w * shift2[:, None], axis=0) + bias_f[u]
        halves2.append(
            extend(
                jnp.concatenate([w * gain2[:, None], w_out[:, u * part : (u + 1) * part].astype(f32)], axis=1),
                jnp.concatenate([bias, jnp.zeros((part,), f32)]),
            )
        )

    head, tail = 2 * hw, 2 * part
    own1, own2 = in_order(halves1), in_order(halves2)
    own1 = after(own1, got[2:])
    near1, far1 = send_near(own1), send(own1, "col", 1)
    near2 = send_near(after(own2, [near1]))
    w1 = [own1, near1, send(near1, "dp", 1), far1]
    far2 = send(after(own2, [far1, w1[2]]), "col", 1)

    base = jnp.arange(half_span, dtype=jnp.int32)
    q_pos = jnp.concatenate([rr * span + core * half_span + base for rr in range(rows)])
    q_start = jnp.where(q_pos >= counts[1], counts[1], jnp.where(q_pos >= counts[0], counts[0], 0))
    frequency = 10000.0 ** (-jnp.arange(ROT // 2, dtype=f32) * 2.0 / ROT)
    angles = (q_pos - q_start).astype(f32)[None, :] * frequency[:, None]
    cosine, sine = jnp.cos(angles), jnp.sin(angles)
    unit, nil = jnp.ones_like(cosine), jnp.zeros_like(sine)
    tables = jnp.stack(
        [
            pick(first_core, cosine, unit),
            pick(first_core, sine, nil),
            pick(first_core, unit, cosine),
            pick(first_core, nil, sine),
        ]
    )

    grid_shape = (cols * block, count)
    xn, cot = call(place_kernel, [shaped(grid_shape, bf16)] * 2, tokens, scalars)
    queries, kv, grad_att = call(
        partial(qkv_kernel, heads),
        [
            shaped((heads, HD, count), bf16),
            shaped((2, heads, HD, count), bf16),
            shaped((heads, HD, count), bf16),
        ],
        [tables, xn, cot, *w1],
        scalars,
    )
    kv_other = [send(kv[:1], "dp", 1), send(kv[1:], "dp", 1)]

    by_head = pl.BlockSpec((1, HD, count), lambda h: (h, 0, 0))
    by_head1 = pl.BlockSpec((1, 1, HD, count), lambda h: (0, h, 0, 0))
    by_head2 = pl.BlockSpec((2, 1, HD, count), lambda h: (0, h, 0, 0))
    attended, grad_q, grad_kv, grad_kv_other = pl.pallas_call(
        partial(attention_kernel, span),
        grid=(heads,),
        in_specs=[
            pl.BlockSpec(memory_space=pltpu.SMEM),
            pl.BlockSpec((1, count), lambda h: (0, 0)),
            by_head,
            by_head2,
            by_head1,
            by_head1,
            by_head,
        ],
        out_specs=[by_head, by_head, by_head2, by_head2],
        out_shape=[
            shaped((heads, HD, count), bf16),
            shaped((heads, HD, count), f32),
            shaped((2, heads, HD, count), f32),
            shaped((2, heads, HD, count), bf16),
        ],
        scratch_shapes=[
            pltpu.VMEM((HD, 2 * count), bf16),
            pltpu.VMEM((HD, 2 * count), bf16),
            pltpu.VMEM((HD, 2 * count), f32),
            pltpu.VMEM((HD, 2 * count), f32),
        ],
        compiler_params=pltpu.CompilerParams(vmem_limit_bytes=48 * 2**20),
        cost_estimate=pl.CostEstimate(
            flops=0, bytes_accessed=0, transcendentals=0
        ),
    )(scalars, q_start[None, :], queries, kv, *kv_other, grad_att)
    grad_kv_got = [send(grad_kv_other[:1], "dp", 1), send(grad_kv_other[1:], "dp", 1)]

    def sums(size):
        return [shaped((block, size), f32)] + [shaped((block, size), bf16)] * 3

    half_act = shaped((head, count), bf16)
    grads_a, att_a, grads_b, att_b, sum1, keep1, give1, far_sum1 = call(
        partial(qkv_grad_kernel, heads),
        [half_act] * 4 + sums(2 * head),
        [tables, grad_q, grad_kv, *grad_kv_got, attended, xn, cot],
        scalars,
    )
    got1 = send(give1, "dp", 1)
    low_near1 = call(pair_kernel, [shaped((block, 2 * head), bf16)], [keep1, got1])[0]
    sum_near1 = send_near(low_near1)
    sum_far1 = send(far_sum1, "col", 1)

    near2, far2 = after([near2, far2], [keep1])
    near2 = after(near2, [far2])
    w2 = [own2, near2, send(near2, "dp", 1), far2]
    act = shaped((part, count), bf16)
    up_a, hid_a, up_b, hid_b, sum2, keep2, give2, far_sum2 = call(
        feed_kernel, [act] * 4 + sums(2 * tail), [after(xn, low_near1), cot, *w2], scalars
    )
    third = 2 * tail // 3
    got2 = [send(give2[:, j * third : (j + 1) * third], "dp", 1) for j in range(3)]
    low_near2 = call(pair_kernel, [shaped((block, 2 * tail), bf16)], [keep2, *got2])[0]

    strip = shaped((cols, 2, width, half_span), bf16)
    sums = call(
        back_kernel,
        [strip] * rows,
        [*w1, *w2, att_a, att_b, grads_a, grads_b, up_a, up_b, hid_a, hid_b],
        scalars,
    )
    low_near2, far_sum2 = after([low_near2, far_sum2], [sum_near1, sum_far1, sums[0]])
    sum_near2 = send_near(low_near2)
    sum_far2 = send(far_sum2, "col", 1)
    sums = after(sums, [sum_near1, sum_far1])
    sums = [sums[0]] + [send(sums[j], "row", j) for j in range(1, rows)]
    piece = shaped((2, width, half_span), bf16)
    back = call(row_kernel, [piece] * cols, [mine, *sums], scalars)
    back, sum_near2, sum_far2 = lax.optimization_barrier((back, sum_near2, sum_far2))
    back = [lax.ppermute(back[k], ("dp", "col"), spread_peers(k, True)) for k in range(4)]
    c_sum = jnp.sum(cotangent.astype(f32), axis=(1, 2))[None]
    total = call(
        total_kernel,
        [shaped((block, 2 * (head + tail)), bf16)],
        [sum_near1, sum_far1, sum1, sum_near2, sum_far2, sum2, c_sum],
    )[0]
    wide = total.astype(f32)
    for k in range(2, dps, 2):
        wide = wide + lax.ppermute(total, "dp", turn_peers(k)).astype(f32)
    total = wide.astype(bf16)
    third = (head + tail) * 2 // 3
    other = [send(total[:, j * third : (j + 1) * third], "dp", 1) for j in range(3)]
    small = call(small_kernel, [shaped((8, width), f32)], [total, *other, own1, own2])[0]
    small = small + send(small, "row", 1)
    small = small + send(small, "row", 2)
    unit = jnp.ones_like(gain1)
    small = small / jnp.stack([gain1, gain1, gain2, gain2, unit, unit, unit, unit])
    scales = jnp.pad(jnp.stack([ln1_gain, ln1_bias, ln2_gain, ln2_bias]), ((0, 4), (0, 0)))
    d_wq, d_wd, d_w_in, d_w_out, d_bq, d_bf = call(
        final_kernel,
        [
            shaped((3, heads, width, HD), f32),
            shaped((heads, width, HD), f32),
            shaped((width, ff), f32),
            shaped((width, ff), f32),
            shaped((3, hw), f32),
            shaped((1, ff), f32),
        ],
        [total, *other, scales],
        scalars,
    )
    back = after(back, d_bf)
    back = swap_by(col, back)
    branch, grad_x = jnp.stack(
        [jnp.concatenate([back[s], back[2 + s]], axis=2) for s in range(2)], axis=2
    ).astype(f32)
    bias_out = b_dense.astype(f32) + b_out.astype(f32)
    layer_out = (hidden_in.astype(f32) + branch + bias_out[:, None, None]).astype(bf16)
    grad_in = cotangent.astype(f32) + grad_x

    return (
        layer_out,
        grad_in,
        d_wq.reshape(w_qkv.shape),
        d_bq,
        d_wd.reshape(w_dense.shape),
        small[4],
        small[0],
        small[1],
        small[2],
        small[3],
        d_w_in,
        d_bf.reshape(ff),
        d_w_out,
        small[5],
    )


def solution(mesh):
    placed = (
        P("col", "dp", "row"),
        P("dp", None),
        P(None, "row", "col"),
        P(None, "row"),
        P("row", "col"),
        P("col"),
        P("col"),
        P("col"),
        P("col"),
        P("col"),
        P("col", "row"),
        P("row"),
        P("col", "row"),
        P("col"),
        P("col", "dp", "row"),
    )
    return jax.shard_map(
        body,
        mesh=mesh,
        in_specs=placed,
        out_specs=(
            P("col", "dp", "row"),
            P("col", "dp", "row"),
            P(None, "row", "col"),
            P(None, "row"),
            P("row", "col"),
            P("col"),
            P("col"),
            P("col"),
            P("col"),
            P("col"),
            P("col", "row"),
            P("row"),
            P("col", "row"),
            P("col"),
        ),
        check_vma=False,
    )
```

```python
from functools import partial

import jax
import jax.numpy as jnp
from jax import lax
from jax.experimental import pallas as pl
from jax.experimental.pallas import tpu as pltpu
from jax.sharding import PartitionSpec as P

D = 768
HD = 64
ROT = 16
EPS = 1e-05
PAD = 16

f32 = jnp.float32
bf16 = jnp.bfloat16


def xor_peers(axis, shift):
    return [(i, i ^ shift) for i in range(lax.axis_size(axis))]


def turn_peers(shift):
    count = lax.axis_size("dp")
    return [(i, (i + shift) % count) for i in range(count)]


def send(x, axis, shift):
    return lax.ppermute(x, axis, xor_peers(axis, shift))


def send_near(x):
    pairs = []
    cols = lax.axis_size("col")
    for dp in range(lax.axis_size("dp")):
        pairs += [(dp * cols + c, dp * cols + (c ^ (3 - dp % 2))) for c in range(cols)]
    return lax.ppermute(x, ("dp", "col"), pairs)


def gather_xor(x, axis):
    return [x] + [send(x, axis, k) for k in range(1, lax.axis_size(axis))]


def after(x, others):
    return lax.optimization_barrier((x, others))[0]


def spread_peers(round_of, back=False):
    pairs = []
    cols = lax.axis_size("col")
    for dp in range(lax.axis_size("dp")):
        for col in range(cols):
            half, seq = divmod(col ^ round_of, 2)
            target = (dp // 2 * 2 + half) * cols + 2 * (dp % 2) + seq
            pairs.append((dp * cols + col, target))
    return [(b, a) for a, b in pairs] if back else pairs


def pick(flag, first, second):
    return jnp.where(flag, first, second)


def swap_by(code, parts):
    parts = [pick((code & 1) == 1, parts[j ^ 1], parts[j]) for j in range(4)]
    return [pick((code & 2) == 2, parts[j ^ 2], parts[j]) for j in range(4)]


def sum_parts(parts):
    total = parts[0].astype(f32)
    for part in parts[1:]:
        total = total + part.astype(f32)
    return total


def dot(a, b, contract):
    return lax.dot_general(a, b, (contract, ((), ())), preferred_element_type=f32)


def extend(columns, bias):
    high = lax.reduce_precision(bias, 8, 7)
    rows = jnp.stack([high, bias - high]).astype(bf16)
    rows = jnp.pad(rows, ((0, PAD - 2), (0, 0)))
    return jnp.concatenate([columns.astype(bf16), rows], axis=0)


def call(kernel, outs, args, scalars=None, scratch=()):
    specs = [pl.BlockSpec(memory_space=pltpu.VMEM) for _ in args]
    if scalars is not None:
        specs = [pl.BlockSpec(memory_space=pltpu.SMEM)] + specs
        args = [scalars, *args]
    return pl.pallas_call(
        kernel,
        out_shape=outs,
        in_specs=specs,
        out_specs=[pl.BlockSpec(memory_space=pltpu.VMEM) for _ in outs],
        compiler_params=pltpu.CompilerParams(vmem_limit_bytes=48 * 2**20),
        scratch_shapes=list(scratch),
        cost_estimate=pl.CostEstimate(flops=0, bytes_accessed=0, transcendentals=0),
    )(*args)


def shaped(shape, dtype):
    return jax.ShapeDtypeStruct(shape, dtype)


def place_kernel(scal, *refs):
    parts, (xn_ref, cot_ref) = refs[:4], refs[4:]
    block = xn_ref.shape[0] // 4
    width, span = parts[0].shape[2:]
    row, crossed = scal[0], scal[2]
    for j in range(4):
        ref = parts[j]
        at = pl.multiple_of((row ^ j) * span, span)
        x = ref[:, 0].astype(f32)
        x = x - jnp.mean(x, axis=(0, 1), keepdims=True)
        x = (x * lax.rsqrt(jnp.mean(x * x, axis=(0, 1), keepdims=True) + EPS)).astype(bf16)
        for k in range(4):
            to = pl.multiple_of((k ^ (2 * crossed)) * block, PAD)
            xn_ref[pl.ds(to, width), pl.ds(at, span)] = x[k]
            cot_ref[pl.ds(to, width), pl.ds(at, span)] = ref[k, 1]
    rest = (lax.broadcasted_iota(jnp.int32, (PAD, xn_ref.shape[1]), 0) < 2).astype(f32).astype(bf16)
    for k in range(4):
        xn_ref[k * block + width : (k + 1) * block, :] = rest
        cot_ref[k * block + width : (k + 1) * block, :] = jnp.zeros_like(rest)


def turn(x, cosine, sine):
    half = ROT // 2
    a, b = x[:half], x[half:ROT]
    return jnp.concatenate([a * cosine - b * sine, b * cosine + a * sine, x[ROT:]], axis=0)


def dot00(a, b):
    return dot(a, b, ((0,), (0,)))


def dot11(a, b):
    return dot(a, b, ((1,), (1,)))


def dot10(a, b):
    return dot(a, b, ((1,), (0,)))


def weight(parts, i, u):
    half = parts[i].shape[1] // 2
    side = 1 - u if i == 2 else u
    return parts[i][:, side * half : (side + 1) * half]


def blocks_of(core, size):
    return [pl.ds(pl.multiple_of(b * size, PAD), size) for b in (0, 3 - core, 2 + core, 1)]


def qkv_kernel(heads, scal, tables, xn, cot, *refs):
    weights, (q_ref, kv_ref, ga_ref) = refs[:4], refs[4:]
    sub = HD // 2
    at_blocks = blocks_of(scal[1], weights[0].shape[0])
    third = heads * sub
    for u in range(2):
        w = [weight(weights, i, u) for i in range(4)]
        pre = sum(dot00(w[i], xn[at_blocks[i], :]) for i in range(4))
        grad = sum(dot00(w[i][:, 2 * 128 :], cot[at_blocks[i], :]) for i in range(4))
        cosine, sine = tables[2 * u], tables[2 * u + 1]
        for h in range(heads):
            dims = slice(u * sub, (u + 1) * sub)
            at = h * sub
            q_ref[h, dims, :] = turn(pre[at : at + sub], cosine, sine).astype(bf16)
            at += third
            kv_ref[0, h, dims, :] = turn(pre[at : at + sub], cosine, sine).astype(bf16)
            at += third
            kv_ref[1, h, dims, :] = pre[at : at + sub].astype(bf16)
            at += third - 2 * 128
            ga_ref[h, dims, :] = grad[at : at + sub].astype(bf16)


def put_sums(refs, i, u, value):
    own, keep, give, far = refs
    half = value.shape[1]
    side = 1 - u if i == 2 else u
    (own, keep, give, far)[i][:, side * half : (side + 1) * half] = value.astype(own.dtype if i == 0 else bf16)


def rows_at(first, *rows):
    at = lax.broadcasted_iota(jnp.int32, (PAD, rows[0].shape[1]), 0)
    return sum(jnp.where(at == first + i, row, 0.0) for i, row in enumerate(rows))


def add_below(ref, rows):
    size = rows.shape[1]
    ref[-PAD:, :size] = (ref[-PAD:, :size].astype(f32) + rows).astype(ref.dtype)


def swapped(x):
    sub = HD // 2
    return jnp.concatenate([x[sub:], x[:sub]], axis=0)


def attention_kernel(
    span, scal, start, q_ref, kv_ref, k_other, v_other, ga_ref, att_ref, gq_ref, gkv_ref, gkv_other, kc, vc, gk, gv
):
    count = q_ref.shape[2]
    rows = 2 * count // span
    half = span // 2
    core = scal[1]
    for rr in range(rows):
        mine, lanes = slice(rr * half, (rr + 1) * half), rr * span
        for at, ref, other in ((0, kc, k_other), (1, vc, v_other)):
            ref[:, lanes : lanes + half] = kv_ref[at, 0, :, mine]
            ref[:, lanes + half : lanes + span] = swapped(other[0, 0, :, mine])
    kt, vt = kc[...].T, vc[...].T
    gk[...] = jnp.zeros_like(gk)
    gv[...] = jnp.zeros_like(gv)
    scale = HD ** (-0.5)
    for a in range(rows):
        size = (a + 1) * span
        mine = slice(a * half, (a + 1) * half)
        q, ga = q_ref[0, :, mine], ga_ref[0, :, mine]
        key = lax.broadcasted_iota(jnp.int32, (size, 1), 0)
        at = key % span
        key = key - at + jnp.where((at >= half) == (core == 0), half, 0) + at % half
        query = lax.broadcasted_iota(jnp.int32, (1, half), 1) + (a * span + core * half)
        first = start[:, mine]
        allowed = (key <= query) & (key >= first)
        scores = jnp.where(allowed, dot10(kt[:size], q) * scale, -1000000000.0)
        top = jnp.max(scores, axis=0, keepdims=True)
        exponent = jnp.exp(scores - top)
        probs = exponent * (1.0 / jnp.sum(exponent, axis=0, keepdims=True))
        low = probs.astype(bf16)
        att_ref[0, :, mine] = dot10(vc[:, :size], low).astype(bf16)
        grad = dot10(vt[:size], ga)
        total = jnp.sum(grad * probs, axis=0, keepdims=True)
        grad = (probs * (grad - total) * scale).astype(bf16)
        gq_ref[0, :, mine] = dot10(kc[:, :size], grad)
        gk[:, :size] += dot11(q, grad)
        gv[:, :size] += dot11(ga, low)
    for rr in range(rows):
        mine, lanes = slice(rr * half, (rr + 1) * half), rr * span
        for ref, at in ((gk, 0), (gv, 1)):
            gkv_ref[at, 0, :, mine] = ref[:, lanes : lanes + half]
            gkv_other[at, 0, :, mine] = ref[:, lanes + half : lanes + span].astype(bf16)


def qkv_grad_kernel(heads, scal, tables, gq_ref, gkv_ref, gk_other, gv_other, att_ref, xn, cot, *refs):
    sub = HD // 2
    third = heads * sub
    outs, sums = refs[:4], refs[4:]
    at_blocks = blocks_of(scal[1], sums[0].shape[0])
    zeros = jnp.zeros((third, xn.shape[1]), bf16)
    for u in range(2):
        grads_ref, att_out = outs[2 * u : 2 * u + 2]
        cosine, sine = tables[2 * u], tables[2 * u + 1]
        dims = slice(u * sub, (u + 1) * sub)
        swap = slice((1 - u) * sub, (2 - u) * sub)
        for h in range(heads):
            at = h * sub
            grads_ref[at : at + sub, :] = turn(gq_ref[h, dims, :], cosine, -sine).astype(bf16)
            g = gkv_ref[0, h, dims, :] + gk_other[0, h, swap, :].astype(f32)
            at += third
            grads_ref[at : at + sub, :] = turn(g, cosine, -sine).astype(bf16)
            g = gkv_ref[1, h, dims, :] + gv_other[0, h, swap, :].astype(f32)
            at += third
            grads_ref[at : at + sub, :] = g.astype(bf16)
            at += third
            att_out[at : at + sub, :] = att_ref[h, dims, :]
        grads_ref[3 * third :, :] = zeros
        for s in range(3):
            att_out[s * third : (s + 1) * third, :] = zeros
        for i in range(4):
            total = dot11(xn[at_blocks[i], :], grads_ref[...]) + dot11(cot[at_blocks[i], :], att_out[...])
            put_sums(sums, i, u, total)


def feed_kernel(scal, xn, cot, *refs):
    weights, acts, sums = refs[:4], refs[4:8], refs[8:]
    at_blocks = blocks_of(scal[1], weights[0].shape[0])
    part = acts[0].shape[0]
    for u in range(2):
        up_ref, grad_ref = acts[2 * u : 2 * u + 2]
        w = [weight(weights, i, u) for i in range(4)]
        pre = sum(dot00(w[i][:, :part], xn[at_blocks[i], :]) for i in range(4))
        phi = 0.5 * (1.0 + lax.erf(pre * (0.5**0.5)))
        slope = phi + pre * (jnp.exp(-0.5 * pre * pre) * 0.3989422804014327)
        up_ref[...] = (pre * phi).astype(bf16)
        grad = sum(dot00(w[i][:, part:], cot[at_blocks[i], :]) for i in range(4))
        grad_ref[...] = (grad * slope).astype(bf16)
        for i in range(4):
            total = [dot11(xn[at_blocks[i], :], grad_ref[...]), dot11(cot[at_blocks[i], :], up_ref[...])]
            put_sums(sums, i, u, jnp.concatenate(total, axis=1))


def back_kernel(scal, *refs):
    w1, w2, acts, outs, held = refs[:4], refs[4:8], refs[8:16], refs[16:-1], refs[-1]
    part = acts[4].shape[0]
    _, _, width, span = outs[0].shape
    row, core = scal[0], scal[1]
    for i, to in enumerate((0, 3 - core, 2 + core, 1)):
        for way in range(2):
            side = slice((1 - way) * part, (2 - way) * part)
            used = slice(2 * 128 * (1 - way), acts[0].shape[0])
            total = sum(dot10(weight(w1, i, u)[:, used], acts[2 * way + u][used, :]) for u in range(2))
            total += sum(dot10(weight(w2, i, u)[:, side], acts[4 + 2 * way + u][...]) for u in range(2))
            held[way] = total[:width].astype(bf16)
            for j, out in enumerate(outs):
                out[to, way] = held[way, :, pl.ds(pl.multiple_of((row ^ j) * span, span), span)]


def pair_kernel(keep, *refs):
    near, size = refs[-1], refs[0].shape[1]
    for j, got in enumerate(refs[:-1]):
        cols = slice(j * size, (j + 1) * size)
        near[:, cols] = (keep[:, cols].astype(f32) + got[...].astype(f32)).astype(bf16)


def total_kernel(near1, far1, own1, near2, far2, own2, c_sum, out):
    at = own1.shape[1]
    out[:, :at] = (near1[...].astype(f32) + far1[...].astype(f32) + own1[...]).astype(bf16)
    out[:, at:] = (near2[...].astype(f32) + far2[...].astype(f32) + own2[...]).astype(bf16)
    add_below(out, rows_at(4, c_sum[...]))


def halves_of(here, there, at, size):
    def theirs(cols):
        piece = there[cols // there[0].shape[1]]
        cols = cols % there[0].shape[1]
        return piece[:, cols : cols + size].astype(f32)

    mine = here[:, at : at + size].astype(f32) + theirs(at + size)
    return mine, here[:, at + size : at + 2 * size].astype(f32) + theirs(at)


def small_kernel(here, there0, there1, there2, own1, own2, out):
    there = (there0, there1, there2)
    width = out.shape[1]
    rows, at = [], 0
    for own, used in ((own1, 3 * own1.shape[1] // 8), (own2, own2.shape[1] // 4)):
        half = own.shape[1] // 2
        gain = bias = 0.0
        for u, m in enumerate(halves_of(here, there, at, half)):
            w = own[:width, u * half : u * half + used]
            ones = jnp.ones((8, used), bf16)
            gain += dot11(ones, (m[:width, :used] * w.astype(f32)).astype(bf16))
            bias += dot11(jnp.broadcast_to(m[width : width + 1, :used], ones.shape).astype(bf16), w)
        rows += [gain[:1], bias[:1]]
        at += 2 * half
    cols = slice(0, width)
    shared = here[width:, cols].astype(f32)[4:5] + there0[width:, cols].astype(f32)[4:5]
    out[...] = jnp.concatenate(rows + [shared, shared, jnp.zeros((2, width), f32)], axis=0)


def final_kernel(scal, here, there0, there1, there2, scales, d_wq, d_wd, d_win, d_wout, d_bq, d_bf):
    there = (there0, there1, there2)
    heads, width, _ = d_wd.shape
    sub = HD // 2
    tail = d_win.shape[1]
    part = tail // 2
    third = heads * sub
    core = scal[1]
    at = lax.broadcasted_iota(jnp.int32, (8, 128), 0)
    eye = (at == lax.broadcasted_iota(jnp.int32, (8, 128), 1)).astype(f32).astype(bf16)
    columns = dot00(scales[...], eye)
    gain1, shift1, gain2, shift2 = (columns[:, i : i + 1] for i in range(4))

    def in_order(pair):
        mine, theirs = pair
        return jnp.where(core == 0, mine, theirs), jnp.where(core == 0, theirs, mine)

    for a, m in enumerate(in_order(halves_of(here, there, 0, 4 * third))):
        dims = slice(a * sub, (a + 1) * sub)
        row = m[width : width + 1, : 3 * third]
        grad = m[:width, : 3 * third] * gain1 + shift1 * row
        for s in range(3):
            for h in range(heads):
                at = (s * heads + h) * sub
                d_wq[s, h, :, dims] = grad[:, at : at + sub]
                d_bq[s : s + 1, h * HD + a * sub : h * HD + (a + 1) * sub] = row[:, at : at + sub]
        for h in range(heads):
            at = 3 * third + h * sub
            d_wd[h, :, dims] = m[:width, at : at + sub]
    for a, m in enumerate(in_order(halves_of(here, there, 8 * third, tail))):
        cols = slice(a * part, (a + 1) * part)
        row = m[width : width + 1, :part]
        d_bf[:, cols] = row
        d_win[:, cols] = m[:width, :part] * gain2 + shift2 * row
        d_wout[:, cols] = m[:width, part:]


def row_kernel(scal, x_ref, *refs):
    parts, outs = refs[:4], refs[4:]
    crossed = scal[2]
    x = x_ref[:, 0].astype(f32)
    x = x - jnp.mean(x, axis=(0, 1), keepdims=True)
    rstd = lax.rsqrt(jnp.mean(x * x, axis=(0, 1), keepdims=True) + EPS)
    x = x * rstd
    sums = []
    for way in range(2):
        total = sum(p[:, way].astype(f32) for p in parts)
        sums.append([jnp.where(crossed == 1, total[k ^ 2], total[k]) for k in range(4)])
    grad = jnp.stack(sums[1])
    grad = rstd * (
        grad
        - jnp.mean(grad, axis=(0, 1), keepdims=True)
        - x * jnp.mean(grad * x, axis=(0, 1), keepdims=True)
    )
    for k in range(4):
        outs[k][0] = sums[0][k].astype(bf16)
        outs[k][1] = grad[k].astype(bf16)


def body(
    hidden_in,
    segments,
    w_qkv,
    b_qkv,
    w_dense,
    b_dense,
    ln1_gain,
    ln1_bias,
    ln2_gain,
    ln2_bias,
    w_in,
    b_in,
    w_out,
    b_out,
    cotangent,
):
    width, seqs, span = hidden_in.shape
    half_span = span // 2
    cols, rows, dps = lax.axis_size("col"), lax.axis_size("row"), lax.axis_size("dp")
    heads = w_qkv.shape[1]
    hw = heads * HD
    sub = HD // 2
    ff = w_in.shape[1]
    core = lax.axis_index("dp") % 2
    row = lax.axis_index("row")
    col = lax.axis_index("col")
    first_core = core == 0
    crossed = (core ^ (col >> 1)) == 1
    block = width + PAD
    count = rows * half_span

    counts = jnp.stack([jnp.sum(segments < 1, axis=1), jnp.sum(segments < 2, axis=1)], axis=1)
    counts = jnp.stack([counts // 256, counts % 256], axis=2).reshape(seqs, 4).astype(bf16)
    counts = jnp.pad(counts[:, None], ((0, 0), (0, PAD - 1), (0, half_span - 4)))
    pieces = []
    for j in range(4):
        at, where = j % 2, slice((j // 2) * half_span, (j // 2 + 1) * half_span)
        pieces.append(jnp.concatenate([hidden_in[:, at, where], cotangent[:, at, where], counts[at]]))
    sent = swap_by(col, pieces)
    got = [lax.ppermute(sent[k], ("dp", "col"), spread_peers(k)) for k in range(4)]
    counts = got[0][2 * width, :4].astype(jnp.int32)
    counts = [256 * counts[0] + counts[1], 256 * counts[2] + counts[3]]
    mine = jnp.stack([g[: 2 * width].reshape(2, width, half_span) for g in got])
    tokens = gather_xor(mine, "row")

    scalars = jnp.stack([row, core, crossed.astype(jnp.int32)])

    gain1, shift1 = ln1_gain.astype(f32), ln1_bias.astype(f32)
    gain2, shift2 = ln2_gain.astype(f32), ln2_bias.astype(f32)

    def in_order(halves):
        low, high = halves
        return jnp.concatenate([pick(first_core, low, high), pick(first_core, high, low)], axis=-1)

    wq = w_qkv.reshape(3, heads, width, 2, sub).transpose(3, 2, 0, 1, 4).reshape(2, width, -1)
    wd = w_dense.reshape(heads, width, 2, sub).transpose(2, 1, 0, 3).reshape(2, width, -1)
    bias_q = b_qkv.reshape(3, heads, 2, sub).transpose(2, 0, 1, 3).reshape(2, -1).astype(f32) / cols
    part = ff // 2
    bias_f = b_in.reshape(2, part).astype(f32) / cols
    halves1, halves2 = [], []
    for u in range(2):
        w = wq[u].astype(f32)
        bias = jnp.sum(w * shift1[:, None], axis=0) + bias_q[u]
        halves1.append(
            extend(
                jnp.concatenate([w * gain1[:, None], wd[u].astype(f32)], axis=1),
                jnp.concatenate([bias, jnp.zeros((heads * sub,), f32)]),
            )
        )
        w = w_in[:, u * part : (u + 1) * part].astype(f32)
        bias = jnp.sum(w * shift2[:, None], axis=0) + bias_f[u]
        halves2.append(
            extend(
                jnp.concatenate([w * gain2[:, None], w_out[:, u * part : (u + 1) * part].astype(f32)], axis=1),
                jnp.concatenate([bias, jnp.zeros((part,), f32)]),
            )
        )

    head, tail = 2 * hw, 2 * part
    own1, own2 = in_order(halves1), in_order(halves2)
    own1 = after(own1, got[2:])
    near1, far1 = send_near(own1), send(own1, "col", 1)
    near2 = send_near(after(own2, [near1]))
    w1 = [own1, near1, send(near1, "dp", 1), far1]
    far2 = send(after(own2, [far1, w1[2]]), "col", 1)

    base = jnp.arange(half_span, dtype=jnp.int32)
    q_pos = jnp.concatenate([rr * span + core * half_span + base for rr in range(rows)])
    q_start = jnp.where(q_pos >= counts[1], counts[1], jnp.where(q_pos >= counts[0], counts[0], 0))
    frequency = 10000.0 ** (-jnp.arange(ROT // 2, dtype=f32) * 2.0 / ROT)
    angles = (q_pos - q_start).astype(f32)[None, :] * frequency[:, None]
    cosine, sine = jnp.cos(angles), jnp.sin(angles)
    unit, nil = jnp.ones_like(cosine), jnp.zeros_like(sine)
    tables = jnp.stack(
        [
            pick(first_core, cosine, unit),
            pick(first_core, sine, nil),
            pick(first_core, unit, cosine),
            pick(first_core, nil, sine),
        ]
    )

    grid_shape = (cols * block, count)
    xn, cot = call(place_kernel, [shaped(grid_shape, bf16)] * 2, tokens, scalars)
    queries, kv, grad_att = call(
        partial(qkv_kernel, heads),
        [
            shaped((heads, HD, count), bf16),
            shaped((2, heads, HD, count), bf16),
            shaped((heads, HD, count), bf16),
        ],
        [tables, xn, cot, *w1],
        scalars,
    )
    kv_other = [send(kv[:1], "dp", 1), send(kv[1:], "dp", 1)]

    by_head = pl.BlockSpec((1, HD, count), lambda h: (h, 0, 0))
    by_head1 = pl.BlockSpec((1, 1, HD, count), lambda h: (0, h, 0, 0))
    by_head2 = pl.BlockSpec((2, 1, HD, count), lambda h: (0, h, 0, 0))
    attended, grad_q, grad_kv, grad_kv_other = pl.pallas_call(
        partial(attention_kernel, span),
        grid=(heads,),
        in_specs=[
            pl.BlockSpec(memory_space=pltpu.SMEM),
            pl.BlockSpec((1, count), lambda h: (0, 0)),
            by_head,
            by_head2,
            by_head1,
            by_head1,
            by_head,
        ],
        out_specs=[by_head, by_head, by_head2, by_head2],
        out_shape=[
            shaped((heads, HD, count), bf16),
            shaped((heads, HD, count), f32),
            shaped((2, heads, HD, count), f32),
            shaped((2, heads, HD, count), bf16),
        ],
        scratch_shapes=[
            pltpu.VMEM((HD, 2 * count), bf16),
            pltpu.VMEM((HD, 2 * count), bf16),
            pltpu.VMEM((HD, 2 * count), f32),
            pltpu.VMEM((HD, 2 * count), f32),
        ],
        compiler_params=pltpu.CompilerParams(vmem_limit_bytes=48 * 2**20),
        cost_estimate=pl.CostEstimate(
            flops=0, bytes_accessed=0, transcendentals=0
        ),
    )(scalars, q_start[None, :], queries, kv, *kv_other, grad_att)
    grad_kv_got = [send(grad_kv_other[:1], "dp", 1), send(grad_kv_other[1:], "dp", 1)]

    def sums(size):
        return [shaped((block, size), f32)] + [shaped((block, size), bf16)] * 3

    half_act = shaped((head, count), bf16)
    grads_a, att_a, grads_b, att_b, sum1, keep1, give1, far_sum1 = call(
        partial(qkv_grad_kernel, heads),
        [half_act] * 4 + sums(2 * head),
        [tables, grad_q, grad_kv, *grad_kv_got, attended, xn, cot],
        scalars,
    )
    got1 = send(give1, "dp", 1)
    low_near1 = call(pair_kernel, [shaped((block, 2 * head), bf16)], [keep1, got1])[0]
    sum_near1 = send_near(low_near1)
    sum_far1 = send(far_sum1, "col", 1)

    near2, far2 = after([near2, far2], [keep1])
    near2 = after(near2, [far2])
    w2 = [own2, near2, send(near2, "dp", 1), far2]
    act = shaped((part, count), bf16)
    up_a, hid_a, up_b, hid_b, sum2, keep2, give2, far_sum2 = call(
        feed_kernel, [act] * 4 + sums(2 * tail), [after(xn, low_near1), cot, *w2], scalars
    )
    third = 2 * tail // 3
    got2 = [send(give2[:, j * third : (j + 1) * third], "dp", 1) for j in range(3)]
    low_near2 = call(pair_kernel, [shaped((block, 2 * tail), bf16)], [keep2, *got2])[0]

    strip = shaped((cols, 2, width, half_span), bf16)
    sums = call(
        back_kernel,
        [strip] * rows,
        [*w1, *w2, att_a, att_b, grads_a, grads_b, up_a, up_b, hid_a, hid_b],
        scalars,
        scratch=[pltpu.VMEM((2, width, count), bf16)],
    )
    low_near2, far_sum2 = after([low_near2, far_sum2], [sum_near1, sum_far1, sums[0]])
    sum_near2 = send_near(low_near2)
    sum_far2 = send(far_sum2, "col", 1)
    sums = after(sums, [sum_near1, sum_far1])
    sums = [sums[0]] + [send(sums[j], "row", j) for j in range(1, rows)]
    piece = shaped((2, width, half_span), bf16)
    back = call(row_kernel, [piece] * cols, [mine, *sums], scalars)
    back, sum_near2, sum_far2 = lax.optimization_barrier((back, sum_near2, sum_far2))
    back = [lax.ppermute(back[k], ("dp", "col"), spread_peers(k, True)) for k in range(4)]
    c_sum = jnp.sum(cotangent.astype(f32), axis=(1, 2))[None]
    total = call(
        total_kernel,
        [shaped((block, 2 * (head + tail)), bf16)],
        [sum_near1, sum_far1, sum1, sum_near2, sum_far2, sum2, c_sum],
    )[0]
    wide = total.astype(f32)
    for k in range(2, dps, 2):
        wide = wide + lax.ppermute(total, "dp", turn_peers(k)).astype(f32)
    total = wide.astype(bf16)
    third = (head + tail) * 2 // 3
    other = [send(total[:, j * third : (j + 1) * third], "dp", 1) for j in range(3)]
    small = call(small_kernel, [shaped((8, width), f32)], [total, *other, own1, own2])[0]
    small = small + send(small, "row", 1)
    small = small + send(small, "row", 2)
    unit = jnp.ones_like(gain1)
    small = small / jnp.stack([gain1, gain1, gain2, gain2, unit, unit, unit, unit])
    scales = jnp.pad(jnp.stack([ln1_gain, ln1_bias, ln2_gain, ln2_bias]), ((0, 4), (0, 0)))
    d_wq, d_wd, d_w_in, d_w_out, d_bq, d_bf = call(
        final_kernel,
        [
            shaped((3, heads, width, HD), f32),
            shaped((heads, width, HD), f32),
            shaped((width, ff), f32),
            shaped((width, ff), f32),
            shaped((3, hw), f32),
            shaped((1, ff), f32),
        ],
        [total, *other, scales],
        scalars,
    )
    back = after(back, d_bf)
    back = swap_by(col, back)
    branch, grad_x = jnp.stack(
        [jnp.concatenate([back[s], back[2 + s]], axis=2) for s in range(2)], axis=2
    ).astype(f32)
    bias_out = b_dense.astype(f32) + b_out.astype(f32)
    layer_out = (hidden_in.astype(f32) + branch + bias_out[:, None, None]).astype(bf16)
    grad_in = cotangent.astype(f32) + grad_x

    return (
        layer_out,
        grad_in,
        d_wq.reshape(w_qkv.shape),
        d_bq,
        d_wd.reshape(w_dense.shape),
        small[4],
        small[0],
        small[1],
        small[2],
        small[3],
        d_w_in,
        d_bf.reshape(ff),
        d_w_out,
        small[5],
    )


def solution(mesh):
    placed = (
        P("col", "dp", "row"),
        P("dp", None),
        P(None, "row", "col"),
        P(None, "row"),
        P("row", "col"),
        P("col"),
        P("col"),
        P("col"),
        P("col"),
        P("col"),
        P("col", "row"),
        P("row"),
        P("col", "row"),
        P("col"),
        P("col", "dp", "row"),
    )
    return jax.shard_map(
        body,
        mesh=mesh,
        in_specs=placed,
        out_specs=(
            P("col", "dp", "row"),
            P("col", "dp", "row"),
            P(None, "row", "col"),
            P(None, "row"),
            P("row", "col"),
            P("col"),
            P("col"),
            P("col"),
            P("col"),
            P("col"),
            P("col", "row"),
            P("row"),
            P("col", "row"),
            P("col"),
        ),
        check_vma=False,
    )
```
